256 devices in a mesh: seq: 16 (over z, y_hi), head: 16 (over x, y_lo, core).
Axes of the slice: x: 4, y: 4 (y_hi: 2, y_lo: 2; y = y_hi * 2 + y_lo), z: 8, core: 2. Of those that a mesh axis runs over, the one named last changes fastest.
Arguments:
- queries: bfloat16 [16384, 4096], P('seq', 'head'), may hold values from -40 to 40
- keys: bfloat16 [16384, 4096], P('seq', 'head'), may hold values from -6 to 6
- values: bfloat16 [16384, 4096], P('seq', 'head'), may hold values from -6 to 6
- out_weight: bfloat16 [4096, 4096], P('head'), may hold values from -0.125 to 0.125
- band_mask: int32 [32, 3], P('seq'), may hold values 0 or 1
- summary_positions: int32 [1024], replicated, may hold values from 0 to 16383, as said below
Outputs:
- mixed: bfloat16 [16384, 4096], P('seq', 'head')
- summary: bfloat16 [1024, 4096], P('seq', 'head')
The draws below stay inside these ranges and needn't reach their ends.
Inputs may be any that keep to these rules, and one draw needn't show every extreme that they name: `summary_positions`: 1024 distinct positions in ascending order; positions 0 and 16383 are always among them.
All inputs are finite; a program needn't handle non-finite values. No bound on the sum of `band_mask` on one device may be relied on, other than what follows from the above.
Results may differ from the reference program's by a relative error of at most 0.0057.
Values may be sent and summed in bfloat16 or wider, within the bound.
No kernel may reach another device: no remote copies, remote signals or barrier semaphores. Data moves between devices by JAX's collectives and lax.ppermute only.
A program may use at most 128 MiB of HBM per device.

```python
import math
import jax
import jax.numpy as jnp
from jax import lax

D = 4096
HEADS = 32
HEAD_DIM = 128
BLOCK = 512
TOK_DEV = 1024
TOKENS = 16384
GLOBALS = 1024
NBLK = 32
N_HEAD = 16


def draw_keys(key, part):
    key = jax.random.fold_in(key, 3)
    drawn = jnp.clip(jax.random.normal(key, (TOKENS, HEADS * HEAD_DIM), jnp.float32), -6.0, 6.0)
    return drawn.astype(jnp.bfloat16)


def draw_queries(key, part):
    key = jax.random.fold_in(key, 7)
    drawn = jnp.clip(jax.random.normal(key, (TOKENS, HEADS * HEAD_DIM), jnp.float32), -6.0, 6.0)
    return drawn.astype(jnp.bfloat16)


def draw_summary_positions(key, part):
    key = jax.random.fold_in(key, 11)
    places = jnp.arange(TOKENS, dtype=jnp.int32)
    shard = places // TOK_DEV
    favoured = jax.random.randint(jax.random.fold_in(key, 1), (), 0, 4)
    scores = jax.random.randint(jax.random.fold_in(key, 2), (TOKENS,), 0, 4096)
    scores = scores + 4096 * (shard % 4 == favoured).astype(jnp.int32)
    ends = (places == 0) | (places == TOKENS - 1)
    scores = jnp.where(ends, 8192, scores)
    combined = scores * TOKENS + places
    _, chosen = lax.top_k(combined, GLOBALS)
    return jnp.sort(chosen).astype(jnp.int32)


def plant(values, rng, smallest, high):
    place = [jax.random.randint(jax.random.fold_in(rng, axis), (), 0, length) for axis, length in enumerate(values.shape)]
    main_axis = values.shape.index(max(values.shape))
    beside = place[:main_axis] + [(place[main_axis] + 1) % values.shape[main_axis]] + place[main_axis + 1:]
    return values.at[tuple(place)].set(smallest).at[tuple(beside)].set(high)


def spiked(entries, stream_key, source, target, shards_of, factor):
    def block_of(position):
        return (jnp.arange(entries.shape[position]) // (entries.shape[position] // shards_of)).reshape((-1,) + (1,) * (entries.ndim - 1 - position))

    one_side = jax.random.permutation(stream_key, shards_of)[block_of(target)]
    second = (block_of(target) + shards_of // 2) % shards_of
    return jnp.where((block_of(source) == one_side) | (block_of(source) == second), factor * entries, entries)


def block_scale(own_key, shape, pieces, smallest, largest):
    factor_of, own = 1.0, jax.random.fold_in(own_key, 6)
    for axis_at, parts in pieces:
        draws = jnp.exp(jax.random.uniform(jax.random.fold_in(own, axis_at), (parts,), jnp.float32, smallest / len(pieces), largest / len(pieces)))
        factor_of = factor_of * jnp.repeat(draws, shape[axis_at] // parts).reshape([-1 if axis == axis_at else 1 for axis in range(len(shape))])
    return factor_of


def gaussian(stream_key, extent, deviation, reach, pieces=(), kind=jnp.bfloat16):
    values = deviation * jax.random.normal(stream_key, extent, jnp.float32)
    if pieces:
        values = values * block_scale(stream_key, extent, pieces, -0.22, 0.18)
    return jnp.clip(values, -reach, reach).astype(kind)


def gaussian_with(own_key, dims, spread, most, pieces, heavy, kind=jnp.bfloat16):
    array = spread * jax.random.normal(own_key, dims, jnp.float32)
    if pieces:
        array = array * block_scale(own_key, dims, pieces, -0.22, 0.18)
    return jnp.clip(spiked(array, jax.random.fold_in(own_key, 3), *heavy), -most, most).astype(kind)


def setup_inputs(seed: int = 0) -> dict:
    seeds = jax.random.split(jax.random.key(seed), 7)
    queries = draw_queries(jax.random.fold_in(seeds[6], 71), 0)
    keys = draw_keys(jax.random.fold_in(seeds[6], 71), 0)
    values = gaussian(seeds[2], (TOKENS, HEADS * HEAD_DIM), 1.0, 6.0, ((0, 16), (1, 16)))
    out_weight = gaussian_with(seeds[3], (HEADS * HEAD_DIM, D), (HEADS * HEAD_DIM) ** -0.5, 0.125, ((0, 16),), (0, 1, 16, 2.0))
    band_mask = plant((jax.random.randint(seeds[4], (NBLK, 3), 0, 3) < 2).astype(jnp.int32), jax.random.fold_in(seeds[4], 1), 0, 1)
    summary_positions = draw_summary_positions(jax.random.fold_in(seeds[6], 71), 0)
    return {"queries": queries, "keys": keys, "values": values, "out_weight": out_weight, "band_mask": band_mask, "summary_positions": summary_positions}


def attend_keys(query_rows, key_rows, value_rows, live, scale):
    count = query_rows.shape[0]
    heads_all = query_rows.shape[1] // HEAD_DIM
    query_heads = query_rows.reshape(count, heads_all, HEAD_DIM).astype(jnp.float32)
    key_heads = key_rows.reshape(key_rows.shape[0], heads_all, HEAD_DIM).astype(jnp.float32)
    value_heads = value_rows.reshape(value_rows.shape[0], heads_all, HEAD_DIM).astype(jnp.float32)
    scores = jnp.einsum('qhd,khd->hqk', query_heads, key_heads) * scale
    scores = jnp.where(live[None, None, :], scores, -jnp.inf)
    peak = lax.optimization_barrier(jnp.max(scores, axis=-1, keepdims=True))
    weights = jnp.exp(scores - peak)
    totals = lax.optimization_barrier(jnp.sum(weights, axis=-1))
    probs = lax.optimization_barrier(weights.astype(jnp.bfloat16)).astype(jnp.float32)
    summed = jnp.einsum('hqk,khd->qhd', probs, value_heads)
    result = summed / jnp.transpose(totals)[:, :, None]
    return result.reshape(count, heads_all * HEAD_DIM).astype(jnp.bfloat16)

def project(rows, out_weight):
    count = rows.shape[0]
    group = rows.shape[1] // N_HEAD
    row_groups = jnp.transpose(rows.reshape(count, N_HEAD, group), (1, 0, 2))
    weight_groups = out_weight.reshape(N_HEAD, group, out_weight.shape[1])

    def add_group(total, operands):
        part = jnp.dot(operands[0], operands[1], preferred_element_type=jnp.float32)
        return (total + part, None)
    start = jnp.zeros((count, out_weight.shape[1]), jnp.float32)
    total, _ = lax.scan(add_group, start, (row_groups, weight_groups))
    return total.astype(jnp.bfloat16)

def reference(queries, keys, values, out_weight, band_mask, summary_positions):
    scale = jnp.float32(1.0 / math.sqrt(HEAD_DIM))
    width = HEADS * HEAD_DIM
    padding = jnp.zeros((BLOCK, width), jnp.bfloat16)
    keys_padded = jnp.concatenate([padding, keys, padding], axis=0)
    values_padded = jnp.concatenate([padding, values, padding], axis=0)
    summary_queries = jnp.take(queries, summary_positions, axis=0)
    summary_keys = jnp.take(keys, summary_positions, axis=0)
    summary_values = jnp.take(values, summary_positions, axis=0)
    summary_blocks = summary_positions // BLOCK
    offsets = jnp.arange(3, dtype=jnp.int32) - 1

    def attend_block(block_index):
        start = (block_index * BLOCK).astype(jnp.int32)
        query_rows = lax.dynamic_slice_in_dim(queries, start, BLOCK, 0)
        band_keys = lax.dynamic_slice_in_dim(keys_padded, start, 3 * BLOCK, 0)
        band_values = lax.dynamic_slice_in_dim(values_padded, start, 3 * BLOCK, 0)
        neighbour = block_index + offsets
        exists = (neighbour >= 0) & (neighbour < NBLK)
        band_live = (band_mask[block_index] == 1) & exists
        relative = summary_blocks - block_index
        hits = (relative[:, None] == offsets[None, :]) & band_live[None, :]
        global_live = jnp.logical_not(jnp.any(hits, axis=1))
        live = jnp.concatenate([jnp.repeat(band_live, BLOCK), global_live])
        all_keys = jnp.concatenate([band_keys, summary_keys], axis=0)
        all_values = jnp.concatenate([band_values, summary_values], axis=0)
        return attend_keys(query_rows, all_keys, all_values, live, scale)
    attended = lax.map(attend_block, jnp.arange(NBLK, dtype=jnp.int32)).reshape(TOKENS, width)
    head_queries = jnp.transpose(summary_queries.reshape(GLOBALS, HEADS, HEAD_DIM), (1, 0, 2))
    head_keys = jnp.transpose(keys.reshape(TOKENS, HEADS, HEAD_DIM), (1, 0, 2))
    head_values = jnp.transpose(values.reshape(TOKENS, HEADS, HEAD_DIM), (1, 0, 2))
    every_key = jnp.ones((TOKENS,), dtype=bool)

    def attend_head(operands):
        return attend_keys(operands[0], operands[1], operands[2], every_key, scale)
    per_head = lax.map(attend_head, (head_queries, head_keys, head_values))
    summary_attended = jnp.transpose(per_head, (1, 0, 2)).reshape(GLOBALS, width)
    mixed = project(attended, out_weight)
    summary = project(summary_attended, out_weight)
    return (mixed, summary)
```

```python
import functools
import math

import jax
import jax.numpy as jnp
from jax import lax
from jax.experimental import pallas as pl
from jax.experimental.pallas import tpu as pltpu
from jax.sharding import PartitionSpec as P

HEAD_DIM = 128
BLOCK = 512
NEG = -1e30
F32 = jnp.float32
BF16 = jnp.bfloat16
VMEM = pl.BlockSpec(memory_space=pltpu.VMEM)
SMEM = pl.BlockSpec(memory_space=pltpu.SMEM)
PARAMS = pltpu.CompilerParams(vmem_limit_bytes=50 * 1024 * 1024)


def kernel_call(body, outs, ins, scratch=(), smem=()):
    specs = [SMEM if i in smem else VMEM for i in range(len(ins))]
    return pl.pallas_call(
        body,
        out_shape=outs,
        in_specs=specs,
        out_specs=jax.tree.map(lambda _: VMEM, outs),
        scratch_shapes=list(scratch),
        compiler_params=PARAMS,
    )(*ins)


def dot_nt(a, b):
    return lax.dot_general(a, b, (((1,), (1,)), ((), ())), preferred_element_type=F32)


def dot_nn(a, b):
    return lax.dot_general(a, b, (((1,), (0,)), ((), ())), preferred_element_type=F32)


def extended(cells, sides, width):
    for axis, dim in sides:
        count = lax.axis_size(axis)
        ends = count - 1
        head = lax.slice_in_dim(cells, 0, width, axis=dim)
        tail = lax.slice_in_dim(cells, cells.shape[dim] - width, cells.shape[dim], axis=dim)
        cells = jnp.concatenate(
            [
                lax.ppermute(tail, axis, [(i, (i + 1) % count) for i in range(ends)]),
                cells,
                lax.ppermute(head, axis, [((i + 1) % count, i) for i in range(ends)]),
            ],
            axis=dim,
        )
    return cells


def band_block(
    query_rows, band_keys, band_values, band_live, summary_keys, summary_values, global_live, scale
):
    count = query_rows.shape[0]
    heads_here = query_rows.shape[1] // HEAD_DIM
    globals_all = summary_keys.shape[0]
    query_heads = query_rows.reshape(count, heads_here, HEAD_DIM)
    global_key_heads = summary_keys.reshape(globals_all, heads_here, HEAD_DIM)
    global_value_heads = summary_values.reshape(globals_all, heads_here, HEAD_DIM)
    global_scores = (
        jnp.einsum(
            "qhd,khd->hqk", query_heads, global_key_heads, preferred_element_type=jnp.float32
        )
        * scale
    )
    global_scores = jnp.where(global_live[None, None, :], global_scores, -jnp.inf)
    key_heads = band_keys.reshape(3 * BLOCK, heads_here, HEAD_DIM)
    value_heads = band_values.reshape(3 * BLOCK, heads_here, HEAD_DIM)
    band_scores = (
        jnp.einsum("qhd,khd->hqk", query_heads, key_heads, preferred_element_type=jnp.float32)
        * scale
    )
    band_scores = jnp.where(jnp.repeat(band_live, BLOCK)[None, None, :], band_scores, -jnp.inf)
    peak = jnp.maximum(jnp.max(band_scores, axis=-1), jnp.max(global_scores, axis=-1))
    band_weights = jnp.exp(band_scores - peak[:, :, None])
    global_weights = jnp.exp(global_scores - peak[:, :, None])
    totals = jnp.sum(band_weights, axis=-1) + jnp.sum(global_weights, axis=-1)
    band_probs = band_weights.astype(jnp.bfloat16)
    global_probs = global_weights.astype(jnp.bfloat16)
    summed = jnp.einsum(
        "hqk,khd->qhd", global_probs, global_value_heads, preferred_element_type=jnp.float32
    )
    summed = summed + jnp.einsum(
        "hqk,khd->qhd", band_probs, value_heads, preferred_element_type=jnp.float32
    )
    result = summed / jnp.transpose(totals)[:, :, None]
    return result.reshape(count, heads_here * HEAD_DIM).astype(jnp.bfloat16)


def general(queries, keys, values, out_weight, band_mask, summary_positions, starts):
    tok_rows, width = queries.shape
    heads_here = width // HEAD_DIM
    blocks_here = tok_rows // BLOCK
    seq_count = lax.axis_size("seq")
    seq_rank = lax.axis_index("seq")
    first_token = seq_rank * tok_rows
    total_blocks = seq_count * blocks_here
    globals_all = summary_positions.shape[0]
    glob_rows = globals_all // seq_count
    scale = jnp.float32(1.0 / math.sqrt(HEAD_DIM))
    local_place = summary_positions - first_token
    owned = (local_place >= 0) & (local_place < tok_rows)
    picked_index = jnp.clip(local_place, 0, tok_rows - 1)
    picked_queries = jnp.where(owned[:, None], jnp.take(queries, picked_index, axis=0), 0)
    picked_keys = jnp.where(owned[:, None], jnp.take(keys, picked_index, axis=0), 0)
    picked_values = jnp.where(owned[:, None], jnp.take(values, picked_index, axis=0), 0)
    gathered = (
        lax.psum(picked_queries, "seq").astype(jnp.float32),
        lax.psum(picked_keys, "seq").astype(jnp.float32),
        lax.psum(picked_values, "seq").astype(jnp.float32),
    )
    summary_queries = gathered[0].astype(jnp.bfloat16)
    summary_keys = gathered[1].astype(jnp.bfloat16)
    summary_values = gathered[2].astype(jnp.bfloat16)
    paired = jnp.stack([keys, values], axis=1)
    padded = extended(paired, (("seq", 0),), BLOCK)
    summary_blocks = summary_positions // BLOCK
    offsets = jnp.arange(3, dtype=jnp.int32) - 1
    outputs = []
    for block_index in range(blocks_here):
        query_rows = queries[block_index * BLOCK : (block_index + 1) * BLOCK]
        window = padded[block_index * BLOCK : block_index * BLOCK + 3 * BLOCK]
        my_block = seq_rank * blocks_here + block_index
        neighbour = my_block + offsets
        exists = (neighbour >= 0) & (neighbour < total_blocks)
        band_live = (band_mask[block_index] == 1) & exists
        relative = summary_blocks - my_block
        hits = (relative[:, None] == offsets[None, :]) & band_live[None, :]
        global_live = jnp.logical_not(jnp.any(hits, axis=1))
        outputs.append(
            band_block(
                query_rows,
                window[:, 0],
                window[:, 1],
                band_live,
                summary_keys,
                summary_values,
                global_live,
                scale,
            )
        )
    attended = jnp.concatenate(outputs, axis=0)
    key_heads = keys.reshape(tok_rows, heads_here, HEAD_DIM)
    value_heads = values.reshape(tok_rows, heads_here, HEAD_DIM)
    query_heads = summary_queries.reshape(globals_all, heads_here, HEAD_DIM)
    summary_scores = (
        jnp.einsum("ghd,khd->hgk", query_heads, key_heads, preferred_element_type=jnp.float32)
        * scale
    )
    local_peak = jnp.max(summary_scores, axis=-1)
    summary_peak = lax.pmax(local_peak, "seq")
    summary_weights = jnp.exp(summary_scores - summary_peak[:, :, None])
    part_totals = jnp.transpose(jnp.sum(summary_weights, axis=-1))
    summary_probs = summary_weights.astype(jnp.bfloat16)
    part_sums = jnp.einsum(
        "hgk,khd->ghd", summary_probs, value_heads, preferred_element_type=jnp.float32
    ).reshape(globals_all, width)
    every_sums, every_totals = lax.psum((part_sums, part_totals), "seq")
    own_sums = lax.dynamic_slice_in_dim(every_sums, seq_rank * glob_rows, glob_rows, 0)
    own_totals = lax.dynamic_slice_in_dim(every_totals, seq_rank * glob_rows, glob_rows, 0)
    summary_attended = (
        (own_sums.reshape(glob_rows, heads_here, HEAD_DIM) / own_totals[:, :, None])
        .reshape(glob_rows, width)
        .astype(jnp.bfloat16)
    )
    all_rows = jnp.concatenate([attended, summary_attended], axis=0)
    features = jnp.transpose(
        lax.psum_scatter(
            lax.dot_general(
                out_weight, all_rows, (((0,), (1,)), ((), ())), preferred_element_type=jnp.float32
            ),
            "head",
            scatter_dimension=0,
            tiled=True,
        )
    )
    result = features.astype(jnp.bfloat16)
    return (result[:tok_rows], result[tok_rows:])


GROUP = 4
SLOTS = 80
CODE = 128


def pick_body(place, q, k, v, *refs):
    outs, first_kv, last_kv = refs[:GROUP], refs[GROUP], refs[GROUP + 1]
    rows = q.shape[0]
    width = q.shape[1]
    lanes = lax.broadcasted_iota(jnp.int32, (SLOTS, rows), 1)
    for d in range(GROUP):
        hot = jnp.where(place[d * SLOTS : (d + 1) * SLOTS, :] == lanes, 1.0, 0.0).astype(BF16)
        outs[d][:, :width] = dot_nn(hot, q[...]).astype(BF16)
        outs[d][:, width : 2 * width] = dot_nn(hot, k[...]).astype(BF16)
        outs[d][:, 2 * width :] = dot_nn(hot, v[...]).astype(BF16)
    first_kv[:, :width] = k[:BLOCK, :]
    first_kv[:, width:] = v[:BLOCK, :]
    last_kv[:, :width] = k[rows - BLOCK :, :]
    last_kv[:, width:] = v[rows - BLOCK :, :]


def band_body(factor, live, q, k, v, before, after, acc, stat, ke, ve):
    rows, width = q.shape
    heads = width // HEAD_DIM
    tile = 256
    window = 3 * BLOCK
    ke[:BLOCK, :] = before[:, :width]
    ke[BLOCK : BLOCK + rows, :] = k[...]
    ke[BLOCK + rows :, :] = after[:, :width]
    for h in range(heads):
        src = slice(h * HEAD_DIM, (h + 1) * HEAD_DIM)
        off = slice(width + h * HEAD_DIM, width + (h + 1) * HEAD_DIM)
        dst = slice(2 * h * HEAD_DIM, (2 * h + 1) * HEAD_DIM)
        one = slice((2 * h + 1) * HEAD_DIM, (2 * h + 2) * HEAD_DIM)
        ve[:BLOCK, dst] = before[:, off]
        ve[BLOCK : BLOCK + rows, dst] = v[:, src]
        ve[BLOCK + rows :, dst] = after[:, off]
        ve[:, one] = jnp.ones((ve.shape[0], HEAD_DIM), BF16)

    def step(t, carry):
        block = t // (BLOCK // tile)
        at = pl.multiple_of(t * tile, tile)
        base = pl.multiple_of(block * BLOCK, BLOCK)
        for h in range(heads):
            cols = slice(h * HEAD_DIM, (h + 1) * HEAD_DIM)
            qt = q[pl.ds(at, tile), cols]
            parts = []
            for j in range(3):
                s = dot_nt(qt, ke[pl.ds(base + j * BLOCK, BLOCK), cols]) * factor
                parts.append(jnp.where(live[block, j] == 1, s, NEG))
            peak = functools.reduce(jnp.maximum, [jnp.max(s, axis=1, keepdims=True) for s in parts])
            both = None
            for j in range(3):
                p = jnp.exp2(parts[j] - peak).astype(BF16)
                o = dot_nn(
                    p, ve[pl.ds(base + j * BLOCK, BLOCK), 2 * h * HEAD_DIM : (2 * h + 2) * HEAD_DIM]
                )
                both = o if both is None else both + o
            acc[pl.ds(at, tile), cols] = both[:, :HEAD_DIM]
            stat[pl.ds(at, tile), 2 * h * HEAD_DIM : (2 * h + 1) * HEAD_DIM] = both[:, HEAD_DIM:]
            stat[pl.ds(at, tile), (2 * h + 1) * HEAD_DIM : (2 * h + 2) * HEAD_DIM] = (
                jnp.broadcast_to(peak, (tile, HEAD_DIM))
            )
        return carry

    lax.fori_loop(0, rows // tile, step, 0)


def main_body(factor, pieces, places, q, bias, acc, stat, *refs):
    ins, (out, qg), (wide, kg, vg) = refs[:pieces], refs[pieces : pieces + 2], refs[pieces + 2 :]
    rows, width = q.shape
    heads = width // HEAD_DIM
    total = kg.shape[0]
    tile = 256
    wide[...] = jnp.zeros(wide.shape, F32)
    n = 0
    for ref in ins:
        for b in range(ref.shape[0] // SLOTS):
            at = places[n]
            n += 1
            block = ref[b * SLOTS : (b + 1) * SLOTS, :].astype(F32)
            block = jnp.concatenate([block, jnp.zeros((8, block.shape[1]), F32)], axis=0)
            block = pltpu.roll(block, at % 8, 0)
            wide[pl.ds(pl.multiple_of(at // 8 * 8, 8), SLOTS + 8), :] += block
    qg[...] = wide[:total, :width].astype(BF16)
    kg[...] = wide[:total, width : 2 * width].astype(BF16)
    for h in range(heads):
        vg[:, 2 * h * HEAD_DIM : (2 * h + 1) * HEAD_DIM] = wide[
            :total, 2 * width + h * HEAD_DIM : 2 * width + (h + 1) * HEAD_DIM
        ].astype(BF16)
        vg[:, (2 * h + 1) * HEAD_DIM : (2 * h + 2) * HEAD_DIM] = jnp.ones((total, HEAD_DIM), BF16)

    def step(t, carry):
        block = t // (BLOCK // tile)
        at = pl.multiple_of(t * tile, tile)
        for h in range(heads):
            cols = slice(h * HEAD_DIM, (h + 1) * HEAD_DIM)
            s = dot_nt(q[pl.ds(at, tile), cols], kg[:, cols]) * factor
            s = s + bias[block]
            band_sum = stat[pl.ds(at, tile), 2 * h * HEAD_DIM : (2 * h + 1) * HEAD_DIM]
            band_peak = stat[pl.ds(at, tile), (2 * h + 1) * HEAD_DIM : (2 * h + 2) * HEAD_DIM]
            peak = jnp.maximum(jnp.max(s, axis=1, keepdims=True), band_peak[:, :1])
            p = jnp.exp2(s - peak).astype(BF16)
            o = dot_nn(p, vg[:, 2 * h * HEAD_DIM : (2 * h + 2) * HEAD_DIM])
            back = jnp.exp2(band_peak - peak)
            num = o[:, :HEAD_DIM] + back * acc[pl.ds(at, tile), cols]
            den = o[:, HEAD_DIM:] + back * band_sum
            out[pl.ds(at, tile), cols] = (num / den).astype(BF16)
        return carry

    lax.fori_loop(0, rows // tile, step, 0)


def summary_body(factor, qg, k, v, out, ve):
    rows, width = qg.shape
    heads = width // HEAD_DIM
    tile = 256
    for h in range(heads):
        ve[:, 2 * h * HEAD_DIM : (2 * h + 1) * HEAD_DIM] = v[:, h * HEAD_DIM : (h + 1) * HEAD_DIM]
        ve[:, (2 * h + 1) * HEAD_DIM : (2 * h + 2) * HEAD_DIM] = jnp.ones(
            (ve.shape[0], HEAD_DIM), BF16
        )
    lane = lax.broadcasted_iota(jnp.int32, (tile, CODE), 1)

    def step(t, carry):
        at = pl.multiple_of(t * tile, tile)
        code = jnp.zeros((tile, CODE), F32)
        for h in range(heads):
            cols = slice(h * HEAD_DIM, (h + 1) * HEAD_DIM)
            s = dot_nt(qg[pl.ds(at, tile), cols], k[:, cols]) * factor
            peak = jnp.max(s, axis=1, keepdims=True)
            p = jnp.exp2(s - peak).astype(BF16)
            o = dot_nn(p, ve[:, 2 * h * HEAD_DIM : (2 * h + 2) * HEAD_DIM])
            den = o[:, HEAD_DIM:]
            out[pl.ds(at, tile), cols] = (o[:, :HEAD_DIM] / den).astype(BF16)
            size = peak + jnp.log2(den)
            for piece in range(3):
                part = size.astype(BF16).astype(F32)
                code = jnp.where(lane == 3 * h + piece, part, code)
                size = size - part
        out[pl.ds(at, tile), width:] = code.astype(BF16)
        return carry

    lax.fori_loop(0, rows // tile, step, 0)


def merge_body(sent, out):
    count, rows, full = sent.shape
    width = full - CODE
    for h in range(width // HEAD_DIM):
        cols = slice(h * HEAD_DIM, (h + 1) * HEAD_DIM)
        sizes = []
        for s in range(count):
            code = sent[s, :, width:].astype(F32)
            sizes.append(
                code[:, 3 * h : 3 * h + 1]
                + code[:, 3 * h + 1 : 3 * h + 2]
                + code[:, 3 * h + 2 : 3 * h + 3]
            )
        peak = functools.reduce(jnp.maximum, sizes)
        num = jnp.zeros((rows, HEAD_DIM), F32)
        den = jnp.zeros((rows, 1), F32)
        for s in range(count):
            w = jnp.exp2(sizes[s] - peak)
            num = num + w * sent[s, :, cols].astype(F32)
            den = den + w
        out[:, cols] = (num / den).astype(BF16)


def project_body(layout, weights_count, side, *refs):
    pieces = len(layout)
    ins, weights = refs[:pieces], refs[pieces : pieces + weights_count]
    mine, other = refs[pieces + weights_count :]
    width = mine.shape[1]
    me = side[0]
    bands = {}
    for i, (first, count, w) in enumerate(layout):
        bands.setdefault((first, count), [])
    edges = sorted({f for f, c, w in layout} | {f + c for f, c, w in layout})
    for out, who in ((mine, me), (other, 1 - me)):
        cols = pl.ds(pl.multiple_of(who * width, width), width)
        for low, high in zip(edges[:-1], edges[1:]):
            total = None
            for i, (first, count, w) in enumerate(layout):
                if first <= low and high <= first + count:
                    part = dot_nn(ins[i][low - first : high - first, :], weights[w][:, cols])
                    total = part if total is None else total + part
            out[low:high, :] = total


def balanced(queries, keys, values, out_weight, band_mask, positions, starts):
    rows, width = queries.shape
    seq_count = lax.axis_size("seq")
    head_count = lax.axis_size("head")
    rank = lax.axis_index("seq")
    place = lax.axis_index("head")
    blocks = rows // BLOCK
    total = positions.shape[0]
    home_rows = total // seq_count
    first = rank * rows
    factor = (1.0 / math.sqrt(HEAD_DIM)) * math.log2(math.e)
    shape = jax.ShapeDtypeStruct

    def seq_pp(x, f):
        return lax.ppermute(x, "seq", [(i, f(i) % seq_count) for i in range(seq_count)])

    def head_pp(x, f):
        return lax.ppermute(x, "head", [(i, f(i) % head_count) for i in range(head_count)])

    group, member = rank // GROUP, rank % GROUP
    begin = starts[group]
    count = starts[group + 1] - begin
    order = member ^ jnp.arange(GROUP, dtype=jnp.int32)
    slot = (order[:, None] * SLOTS + jnp.arange(SLOTS, dtype=jnp.int32)[None, :]).reshape(-1)
    padded = jnp.concatenate([positions, jnp.zeros((GROUP * SLOTS,), jnp.int32)])
    wanted = jnp.where(slot < count, jnp.take(padded, begin + slot) - first, -1)[:, None]
    pick = shape((SLOTS, 3 * width), BF16)
    edge = shape((BLOCK, 2 * width), BF16)
    *picked, first_kv, last_kv = kernel_call(
        pick_body, [pick] * GROUP + [edge, edge], [wanted, queries, keys, values]
    )
    home = picked[0]
    for d in range(1, GROUP):
        home = home + seq_pp(picked[d], lambda i: i ^ d)
    pair = jnp.concatenate([home, seq_pp(home, lambda i: i ^ 1)], axis=0)
    up = lambda x: seq_pp(x, lambda i: i + 2)
    down = lambda x: seq_pp(x, lambda i: i - 2)
    a1, b1 = up(pair), down(pair)
    a2, b2 = up(a1), down(b1)
    a3, b3 = up(a2), down(b2)
    a4, b4 = up(a3[:SLOTS]), down(b3[SLOTS:])
    pieces = [pair, a1, b1, a2, b2, a3, b3, a4, b4]
    steps = [0, -1, 1, -2, 2, -3, 3, -4]
    owners = []
    for d in steps:
        owners += [rank + 2 * d, (rank ^ 1) + 2 * d]
    owners = jnp.stack(owners) % seq_count
    places = jnp.take(starts, owners // GROUP) + SLOTS * (owners % GROUP)

    before = seq_pp(last_kv, lambda i: i + 1)
    after = seq_pp(first_kv, lambda i: i - 1)
    offsets = jnp.arange(3, dtype=jnp.int32) - 1
    my_block = rank * blocks + jnp.arange(blocks, dtype=jnp.int32)
    neighbour = my_block[:, None] + offsets[None, :]
    live = (band_mask == 1) & (neighbour >= 0) & (neighbour < seq_count * blocks)
    relative = (positions // BLOCK)[None, :] - my_block[:, None]
    hits = (relative[:, None, :] == offsets[None, :, None]) & live[:, :, None]
    bias = jnp.where(jnp.any(hits, axis=1), jnp.float32(NEG), jnp.float32(0.0))[:, None, :]
    acc, stat = kernel_call(
        functools.partial(band_body, factor),
        [shape((rows, width), F32), shape((rows, 2 * width), F32)],
        [live.astype(jnp.int32), queries, keys, values, before, after],
        [pltpu.VMEM((rows + 2 * BLOCK, width), BF16), pltpu.VMEM((rows + 2 * BLOCK, 2 * width), BF16)],
        smem=(0,),
    )

    chips = head_count // 2
    chip, core = place // 2, place % 2
    cx, cy = chip // 2, chip % 2
    by_chip = out_weight.reshape(width, chips, 2 * width)

    def weight_from(dx, dy):
        to = ((cx + dx) % 4) * 2 + (cy ^ dy)
        part = lax.dynamic_index_in_dim(by_chip, to, axis=1, keepdims=False)
        if dx == 0 and dy == 0:
            return part
        return head_pp(part, lambda i: ((i + 4 * dx) % 16) ^ (2 * dy))

    weights = [weight_from(dx, dy) for dy in range(2) for dx in range(4)]

    attended, summary_queries = kernel_call(
        functools.partial(main_body, factor, len(pieces)),
        [shape((rows, width), BF16), shape((total, width), BF16)],
        [places, queries, bias, acc, stat] + pieces,
        [
            pltpu.VMEM((total + GROUP * SLOTS + 8, 3 * width), F32),
            pltpu.VMEM((total, width), BF16),
            pltpu.VMEM((total, 2 * width), BF16),
        ],
        smem=(0,),
    )

    xu = lambda x: head_pp(x, lambda i: i + 4)
    xd = lambda x: head_pp(x, lambda i: i - 4)
    yy = lambda x: head_pp(x, lambda i: i ^ 2)
    half = rows // 2
    layout, parts = [], []

    def around(block, dy):
        u1, d1 = xu(block), xd(block)
        u2, d2 = xu(u1[:half]), xd(d1[half:])
        for piece, at, size, dx in (
            (block, 0, rows, 0),
            (u1, 0, rows, 1),
            (d1, 0, rows, 3),
            (u2, 0, half, 2),
            (d2, half, half, 2),
        ):
            parts.append(piece)
            layout.append((at, size, 4 * dy + dx))

    across = yy(attended)
    around(attended, 0)
    around(across, 1)

    partial = kernel_call(
        functools.partial(summary_body, factor),
        shape((total, width + CODE), BF16),
        [summary_queries, keys, values],
        [pltpu.VMEM((rows, 2 * width), BF16)],
    )
    sent = lax.all_to_all(
        partial.reshape(seq_count, home_rows, width + CODE), "seq", 0, 0, tiled=True
    )
    own = kernel_call(merge_body, shape((home_rows, width), BF16), [sent])
    own_across = yy(own)
    for block, dy in ((own, 0), (own_across, 1)):
        for dx in range(4):
            parts.append(block if dx == 0 else head_pp(block, lambda i: i + 4 * dx))
            layout.append((rows, home_rows, 4 * dy + dx))

    full = shape((rows + home_rows, width), F32)
    mine, other = kernel_call(
        lambda *refs: project_body(layout, len(weights), refs[0], *refs[1:]),
        [full, full],
        [core[None].astype(jnp.int32)] + parts + weights,
        smem=(0,),
    )
    result = (mine + head_pp(other, lambda i: i ^ 1)).astype(BF16)
    return (result[:rows], result[rows:])


def per_device(queries, keys, values, out_weight, band_mask, summary_positions):
    rows = queries.shape[0]
    seq_count = lax.axis_size("seq")
    edges = jnp.arange(seq_count // GROUP + 1, dtype=jnp.int32) * (GROUP * rows)
    starts = jnp.sum(
        (summary_positions[None, :] < edges[:, None]).astype(jnp.int32), axis=1, dtype=jnp.int32
    )
    fits = jnp.max(starts[1:] - starts[:-1]) <= GROUP * SLOTS
    return lax.cond(
        fits,
        balanced,
        general,
        queries,
        keys,
        values,
        out_weight,
        band_mask,
        summary_positions,
        starts,
    )


def solution(mesh):
    in_specs = (
        P("seq", "head"),
        P("seq", "head"),
        P("seq", "head"),
        P("head", None),
        P("seq", None),
        P(),
    )
    out_specs = (P("seq", "head"), P("seq", "head"))
    return jax.shard_map(
        per_device, mesh=mesh, in_specs=in_specs, out_specs=out_specs, check_vma=False
    )
```

```python
import functools
import math

import jax
import jax.numpy as jnp
from jax import lax
from jax.experimental import pallas as pl
from jax.experimental.pallas import tpu as pltpu
from jax.sharding import PartitionSpec as P

HEAD_DIM = 128
BLOCK = 512
NEG = -1e30
F32 = jnp.float32
BF16 = jnp.bfloat16
VMEM = pl.BlockSpec(memory_space=pltpu.VMEM)
SMEM = pl.BlockSpec(memory_space=pltpu.SMEM)
HBM = pl.BlockSpec(memory_space=pl.ANY)
PARAMS = pltpu.CompilerParams(vmem_limit_bytes=50 * 1024 * 1024)


def kernel_call(body, outs, ins, scratch=(), smem=(), hbm=(), load=()):
    load = tuple(load)
    free = [SMEM if i in smem else HBM if i in hbm or i in load else VMEM for i in range(len(ins))]
    held = [pltpu.VMEM(ins[i].shape, ins[i].dtype) for i in load]
    sems = [pltpu.SemaphoreType.DMA((len(load),))] if load else []

    def run(*refs):
        refs = list(refs)
        if load:
            copies = []
            for n, i in enumerate(load):
                to = refs[len(refs) - len(load) - 1 + n]
                copies.append(pltpu.make_async_copy(refs[i], to, refs[-1].at[n]))
                refs[i] = to
            for copy in copies:
                copy.start()
            for copy in copies:
                copy.wait()
            refs = refs[: len(refs) - len(load) - 1]
        body(*refs)

    return pl.pallas_call(
        run,
        out_shape=outs,
        in_specs=free,
        out_specs=jax.tree.map(lambda _: VMEM, outs),
        scratch_shapes=[*scratch, *held, *sems],
        compiler_params=PARAMS,
    )(*ins)


def dot_nt(a, b):
    return lax.dot_general(a, b, (((1,), (1,)), ((), ())), preferred_element_type=F32)


def dot_nn(a, b):
    return lax.dot_general(a, b, (((1,), (0,)), ((), ())), preferred_element_type=F32)


def extended(cells, sides, width):
    for axis, dim in sides:
        count = lax.axis_size(axis)
        ends = count - 1
        head = lax.slice_in_dim(cells, 0, width, axis=dim)
        tail = lax.slice_in_dim(cells, cells.shape[dim] - width, cells.shape[dim], axis=dim)
        cells = jnp.concatenate(
            [
                lax.ppermute(tail, axis, [(i, (i + 1) % count) for i in range(ends)]),
                cells,
                lax.ppermute(head, axis, [((i + 1) % count, i) for i in range(ends)]),
            ],
            axis=dim,
        )
    return cells


def band_block(
    query_rows, band_keys, band_values, band_live, summary_keys, summary_values, global_live, scale
):
    count = query_rows.shape[0]
    heads_here = query_rows.shape[1] // HEAD_DIM
    globals_all = summary_keys.shape[0]
    query_heads = query_rows.reshape(count, heads_here, HEAD_DIM)
    global_key_heads = summary_keys.reshape(globals_all, heads_here, HEAD_DIM)
    global_value_heads = summary_values.reshape(globals_all, heads_here, HEAD_DIM)
    global_scores = (
        jnp.einsum(
            "qhd,khd->hqk", query_heads, global_key_heads, preferred_element_type=jnp.float32
        )
        * scale
    )
    global_scores = jnp.where(global_live[None, None, :], global_scores, -jnp.inf)
    key_heads = band_keys.reshape(3 * BLOCK, heads_here, HEAD_DIM)
    value_heads = band_values.reshape(3 * BLOCK, heads_here, HEAD_DIM)
    band_scores = (
        jnp.einsum("qhd,khd->hqk", query_heads, key_heads, preferred_element_type=jnp.float32)
        * scale
    )
    band_scores = jnp.where(jnp.repeat(band_live, BLOCK)[None, None, :], band_scores, -jnp.inf)
    peak = jnp.maximum(jnp.max(band_scores, axis=-1), jnp.max(global_scores, axis=-1))
    band_weights = jnp.exp(band_scores - peak[:, :, None])
    global_weights = jnp.exp(global_scores - peak[:, :, None])
    totals = jnp.sum(band_weights, axis=-1) + jnp.sum(global_weights, axis=-1)
    band_probs = band_weights.astype(jnp.bfloat16)
    global_probs = global_weights.astype(jnp.bfloat16)
    summed = jnp.einsum(
        "hqk,khd->qhd", global_probs, global_value_heads, preferred_element_type=jnp.float32
    )
    summed = summed + jnp.einsum(
        "hqk,khd->qhd", band_probs, value_heads, preferred_element_type=jnp.float32
    )
    result = summed / jnp.transpose(totals)[:, :, None]
    return result.reshape(count, heads_here * HEAD_DIM).astype(jnp.bfloat16)


def general(queries, keys, values, out_weight, band_mask, summary_positions, starts):
    tok_rows, width = queries.shape
    heads_here = width // HEAD_DIM
    blocks_here = tok_rows // BLOCK
    seq_count = lax.axis_size("seq")
    seq_rank = lax.axis_index("seq")
    first_token = seq_rank * tok_rows
    total_blocks = seq_count * blocks_here
    globals_all = summary_positions.shape[0]
    glob_rows = globals_all // seq_count
    scale = jnp.float32(1.0 / math.sqrt(HEAD_DIM))
    local_place = summary_positions - first_token
    owned = (local_place >= 0) & (local_place < tok_rows)
    picked_index = jnp.clip(local_place, 0, tok_rows - 1)
    picked_queries = jnp.where(owned[:, None], jnp.take(queries, picked_index, axis=0), 0)
    picked_keys = jnp.where(owned[:, None], jnp.take(keys, picked_index, axis=0), 0)
    picked_values = jnp.where(owned[:, None], jnp.take(values, picked_index, axis=0), 0)
    gathered = (
        lax.psum(picked_queries, "seq").astype(jnp.float32),
        lax.psum(picked_keys, "seq").astype(jnp.float32),
        lax.psum(picked_values, "seq").astype(jnp.float32),
    )
    summary_queries = gathered[0].astype(jnp.bfloat16)
    summary_keys = gathered[1].astype(jnp.bfloat16)
    summary_values = gathered[2].astype(jnp.bfloat16)
    paired = jnp.stack([keys, values], axis=1)
    padded = extended(paired, (("seq", 0),), BLOCK)
    summary_blocks = summary_positions // BLOCK
    offsets = jnp.arange(3, dtype=jnp.int32) - 1
    outputs = []
    for block_index in range(blocks_here):
        query_rows = queries[block_index * BLOCK : (block_index + 1) * BLOCK]
        window = padded[block_index * BLOCK : block_index * BLOCK + 3 * BLOCK]
        my_block = seq_rank * blocks_here + block_index
        neighbour = my_block + offsets
        exists = (neighbour >= 0) & (neighbour < total_blocks)
        band_live = (band_mask[block_index] == 1) & exists
        relative = summary_blocks - my_block
        hits = (relative[:, None] == offsets[None, :]) & band_live[None, :]
        global_live = jnp.logical_not(jnp.any(hits, axis=1))
        outputs.append(
            band_block(
                query_rows,
                window[:, 0],
                window[:, 1],
                band_live,
                summary_keys,
                summary_values,
                global_live,
                scale,
            )
        )
    attended = jnp.concatenate(outputs, axis=0)
    key_heads = keys.reshape(tok_rows, heads_here, HEAD_DIM)
    value_heads = values.reshape(tok_rows, heads_here, HEAD_DIM)
    query_heads = summary_queries.reshape(globals_all, heads_here, HEAD_DIM)
    summary_scores = (
        jnp.einsum("ghd,khd->hgk", query_heads, key_heads, preferred_element_type=jnp.float32)
        * scale
    )
    local_peak = jnp.max(summary_scores, axis=-1)
    summary_peak = lax.pmax(local_peak, "seq")
    summary_weights = jnp.exp(summary_scores - summary_peak[:, :, None])
    part_totals = jnp.transpose(jnp.sum(summary_weights, axis=-1))
    summary_probs = summary_weights.astype(jnp.bfloat16)
    part_sums = jnp.einsum(
        "hgk,khd->ghd", summary_probs, value_heads, preferred_element_type=jnp.float32
    ).reshape(globals_all, width)
    every_sums, every_totals = lax.psum((part_sums, part_totals), "seq")
    own_sums = lax.dynamic_slice_in_dim(every_sums, seq_rank * glob_rows, glob_rows, 0)
    own_totals = lax.dynamic_slice_in_dim(every_totals, seq_rank * glob_rows, glob_rows, 0)
    summary_attended = (
        (own_sums.reshape(glob_rows, heads_here, HEAD_DIM) / own_totals[:, :, None])
        .reshape(glob_rows, width)
        .astype(jnp.bfloat16)
    )
    all_rows = jnp.concatenate([attended, summary_attended], axis=0)
    features = jnp.transpose(
        lax.psum_scatter(
            lax.dot_general(
                out_weight, all_rows, (((0,), (1,)), ((), ())), preferred_element_type=jnp.float32
            ),
            "head",
            scatter_dimension=0,
            tiled=True,
        )
    )
    result = features.astype(jnp.bfloat16)
    return (result[:tok_rows], result[tok_rows:])


GROUP = 4
SLOTS = 160
CODE = 128


def edge_body(k, v, first_kv, last_kv):
    rows, width = k.shape
    first_kv[:, :width] = k[:BLOCK, :]
    first_kv[:, width:] = v[:BLOCK, :]
    last_kv[:, :width] = k[rows - BLOCK :, :]
    last_kv[:, width:] = v[rows - BLOCK :, :]


def cut_body(w, after, out):
    chips, _, width = out.shape
    for c in range(chips):
        out[c, :, :] = w[:, c * width : (c + 1) * width]


def pick_body(rank, positions, q, k, v, *refs):
    outs, column = refs[:2], refs[2]
    rows, width = q.shape
    me = rank[0]
    group, half = me // GROUP, (me % GROUP) // 2
    total = positions.shape[1]
    where = positions[...]
    begin = jnp.sum((where < group * GROUP * rows).astype(F32)).astype(jnp.int32)
    local = jnp.where(
        (where >= group * GROUP * rows) & (where < (group + 1) * GROUP * rows),
        where - me * rows,
        -1,
    )
    wide = jnp.broadcast_to(local, (8, total))
    wide = pltpu.roll(wide, lax.rem(total - begin, total), 1)[:, :384]
    lane = lax.broadcasted_iota(jnp.int32, wide.shape, 1)
    wide = jnp.where(lane < 2 * SLOTS, wide, -1)
    column[...] = jnp.transpose(wide.astype(F32))
    lanes = lax.broadcasted_iota(jnp.int32, (SLOTS, rows), 1).astype(F32)
    for part in range(2):
        at = pl.multiple_of((half ^ part) * SLOTS, 8)
        hot = jnp.where(column[pl.ds(at, SLOTS), :1] == lanes, 1.0, 0.0).astype(BF16)
        for i, ref in enumerate((q, k, v)):
            rows_here = dot_nn(hot, ref[...]).astype(BF16)
            outs[part][:, i * width : (i + 1) * width] = rows_here


def band_body(factor, live, q, k, v, before, after, acc, stat, ke, ve):
    rows, width = q.shape
    heads = width // HEAD_DIM
    tile = 256
    window = 3 * BLOCK
    ke[:BLOCK, :] = before[:, :width]
    ke[BLOCK : BLOCK + rows, :] = k[...]
    ke[BLOCK + rows :, :] = after[:, :width]
    for h in range(heads):
        src = slice(h * HEAD_DIM, (h + 1) * HEAD_DIM)
        off = slice(width + h * HEAD_DIM, width + (h + 1) * HEAD_DIM)
        dst = slice(2 * h * HEAD_DIM, (2 * h + 1) * HEAD_DIM)
        one = slice((2 * h + 1) * HEAD_DIM, (2 * h + 2) * HEAD_DIM)
        ve[:BLOCK, dst] = before[:, off]
        ve[BLOCK : BLOCK + rows, dst] = v[:, src]
        ve[BLOCK + rows :, dst] = after[:, off]
        ve[:, one] = jnp.ones((ve.shape[0], HEAD_DIM), BF16)

    def step(t, carry):
        block = t // (BLOCK // tile)
        at = pl.multiple_of(t * tile, tile)
        base = pl.multiple_of(block * BLOCK, BLOCK)
        code = jnp.zeros((tile, HEAD_DIM), F32)
        lane = lax.broadcasted_iota(jnp.int32, code.shape, 1)
        for h in range(heads):
            cols = slice(h * HEAD_DIM, (h + 1) * HEAD_DIM)
            qt = q[pl.ds(at, tile), cols]
            parts = []
            for j in range(3):
                s = dot_nt(qt, ke[pl.ds(base + j * BLOCK, BLOCK), cols]) * factor
                parts.append(jnp.where(live[block, j] == 1, s, NEG))
            peak = functools.reduce(jnp.maximum, [jnp.max(s, axis=1, keepdims=True) for s in parts])
            both = None
            for j in range(3):
                p = jnp.exp2(parts[j] - peak).astype(BF16)
                o = dot_nn(
                    p, ve[pl.ds(base + j * BLOCK, BLOCK), 2 * h * HEAD_DIM : (2 * h + 2) * HEAD_DIM]
                )
                both = o if both is None else both + o
            acc[pl.ds(at, tile), cols] = both[:, :HEAD_DIM]
            pair = jnp.where(lane == 2 * h, both[:, HEAD_DIM:], peak)
            code = jnp.where(lane // 2 == h, pair, code)
        stat[pl.ds(at, tile), :] = code
        return carry

    lax.fori_loop(0, rows // tile, step, 0, unroll=2)


def gather_body(factor, pieces, places, k, v, *refs):
    ins, (out, kg, vg), (wide, qg, ve) = refs[:pieces], refs[pieces : pieces + 3], refs[pieces + 3 :]
    rows, width = k.shape
    heads = width // HEAD_DIM
    total = kg.shape[0]
    tile = 256
    wide[...] = jnp.zeros(wide.shape, F32)
    for n, ref in enumerate(ins):
        at = places[n]
        block = jnp.concatenate(
            [ref[...].astype(F32), jnp.zeros((8, ref.shape[1]), F32)], axis=0
        )
        block = pltpu.roll(block, at % 8, 0)
        wide[pl.ds(pl.multiple_of(at // 8 * 8, 8), block.shape[0]), :] += block
    qg[...] = wide[:total, :width].astype(BF16)
    kg[...] = wide[:total, width : 2 * width].astype(BF16)
    vg[...] = wide[:total, 2 * width :].astype(BF16)
    for h in range(heads):
        ve[:, 2 * h * HEAD_DIM : (2 * h + 1) * HEAD_DIM] = v[:, h * HEAD_DIM : (h + 1) * HEAD_DIM]
        ve[:, (2 * h + 1) * HEAD_DIM : (2 * h + 2) * HEAD_DIM] = jnp.ones((rows, HEAD_DIM), BF16)
    lane = lax.broadcasted_iota(jnp.int32, (tile, CODE), 1)

    def step(t, carry):
        at = pl.multiple_of(t * tile, tile)
        code = jnp.zeros((tile, CODE), F32)
        for h in range(heads):
            cols = slice(h * HEAD_DIM, (h + 1) * HEAD_DIM)
            s = dot_nt(qg[pl.ds(at, tile), cols], k[:, cols]) * factor
            peak = jnp.max(s, axis=1, keepdims=True)
            p = jnp.exp2(s - peak).astype(BF16)
            o = dot_nn(p, ve[:, 2 * h * HEAD_DIM : (2 * h + 2) * HEAD_DIM])
            den = o[:, HEAD_DIM:]
            out[pl.ds(at, tile), cols] = (o[:, :HEAD_DIM] / den).astype(BF16)
            size = peak + jnp.log2(den)
            for piece in range(3):
                part = size.astype(BF16).astype(F32)
                code = jnp.where(lane == 3 * h + piece, part, code)
                size = size - part
        out[pl.ds(at, tile), width:] = code.astype(BF16)
        return carry

    lax.fori_loop(0, total // tile, step, 0, unroll=2)


def main_body(factor, q, bias, acc, stat, kg, v, sent, out, vg):
    rows, width = q.shape
    heads = width // HEAD_DIM
    total = kg.shape[0]
    tile = 256
    for h in range(heads):
        vg[:, 2 * h * HEAD_DIM : (2 * h + 1) * HEAD_DIM] = v[:, h * HEAD_DIM : (h + 1) * HEAD_DIM]
        vg[:, (2 * h + 1) * HEAD_DIM : (2 * h + 2) * HEAD_DIM] = jnp.ones((total, HEAD_DIM), BF16)

    def step(t, carry):
        block = t // (BLOCK // tile)
        at = pl.multiple_of(t * tile, tile)
        for h in range(heads):
            cols = slice(h * HEAD_DIM, (h + 1) * HEAD_DIM)
            s = dot_nt(q[pl.ds(at, tile), cols], kg[:, cols]) * factor
            s = s + bias[block]
            band_sum = stat[pl.ds(at, tile), 2 * h : 2 * h + 1]
            band_peak = stat[pl.ds(at, tile), 2 * h + 1 : 2 * h + 2]
            peak = jnp.maximum(jnp.max(s, axis=1, keepdims=True), band_peak)
            p = jnp.exp2(s - peak).astype(BF16)
            o = dot_nn(p, vg[:, 2 * h * HEAD_DIM : (2 * h + 2) * HEAD_DIM])
            back = jnp.exp2(band_peak - peak)
            num = o[:, :HEAD_DIM] + back * acc[pl.ds(at, tile), cols]
            den = o[:, HEAD_DIM:] + back * band_sum
            out[pl.ds(at, tile), cols] = (num / den).astype(BF16)
        return carry

    lax.fori_loop(0, rows // tile, step, 0, unroll=2)


def merge_body(sent, out):
    count, rows, full = sent.shape
    width = full - CODE
    for h in range(width // HEAD_DIM):
        cols = slice(h * HEAD_DIM, (h + 1) * HEAD_DIM)
        sizes = []
        for s in range(count):
            code = sent[s, :, width:].astype(F32)
            sizes.append(
                code[:, 3 * h : 3 * h + 1]
                + code[:, 3 * h + 1 : 3 * h + 2]
                + code[:, 3 * h + 2 : 3 * h + 3]
            )
        peak = functools.reduce(jnp.maximum, sizes)
        num = jnp.zeros((rows, HEAD_DIM), F32)
        den = jnp.zeros((rows, 1), F32)
        for s in range(count):
            w = jnp.exp2(sizes[s] - peak)
            num = num + w * sent[s, :, cols].astype(F32)
            den = den + w
        out[:, cols] = (num / den).astype(BF16)


def project_body(layout, flip, side, order, *refs):
    pieces = len(layout)
    ins, weights, mine, other = refs[:pieces], refs[pieces], refs[pieces + 1], refs[pieces + 2]
    x, w, sems = refs[pieces + 3 :]
    rows, width = mine.shape
    copies = []
    chip = side[1] if flip == 0 else 1 - side[1]
    features = pl.ds(pl.multiple_of(chip * 2 * width, 2 * width), 2 * width)
    for d in range(w.shape[0] // width):
        copies.append((weights.at[order[d], :, features], w.at[pl.ds(d * width, width), :]))
    for piece, (first, at) in zip(ins, layout):
        copies.append((piece, x.at[pl.ds(first, piece.shape[0]), pl.ds(at * width, width)]))
    copies = [pltpu.make_async_copy(a, b, sems.at[i]) for i, (a, b) in enumerate(copies)]
    for copy in copies:
        copy.start()
    for copy in copies:
        copy.wait()
    for out, core in ((other, 1 - side[0]), (mine, side[0])):
        cols = pl.ds(pl.multiple_of(core * width, width), width)
        for low in range(0, rows, 256):
            high = min(low + 256, rows)
            out[low:high, :] = dot_nn(x[low:high, :], w[:, cols])


def join_body(a, b, out):
    out[...] = (a[...] + b[...]).astype(BF16)


def final_body(fits, mine, other, across, slow, s_slow, out, s_out):
    count = out.shape[0]

    @pl.when(fits[0] == 1)
    def _():
        total = mine[...] + other[...] + across[...].astype(F32)
        out[...] = total[:count, :].astype(BF16)
        s_out[...] = total[count:, :].astype(BF16)

    @pl.when(fits[0] != 1)
    def _():
        pltpu.sync_copy(slow, out)
        pltpu.sync_copy(s_slow, s_out)


def balanced(queries, keys, values, out_weight, band_mask, positions, starts):
    rows, width = queries.shape
    seq_count = lax.axis_size("seq")
    head_count = lax.axis_size("head")
    rank = lax.axis_index("seq")
    place = lax.axis_index("head")
    blocks = rows // BLOCK
    total = positions.shape[0]
    home_rows = total // seq_count
    factor = (1.0 / math.sqrt(HEAD_DIM)) * math.log2(math.e)
    shape = jax.ShapeDtypeStruct

    def seq_pp(x, f):
        return lax.ppermute(x, "seq", [(i, f(i) % seq_count) for i in range(seq_count)])

    def head_pp(x, f):
        return lax.ppermute(x, "head", [(i, f(i) % head_count) for i in range(head_count)])

    edge = shape((BLOCK, 2 * width), BF16)
    first_kv, last_kv = kernel_call(edge_body, [edge, edge], [keys, values])

    pick = shape((SLOTS, 3 * width), BF16)
    keep, away = kernel_call(
        pick_body,
        [pick, pick],
        [rank[None].astype(jnp.int32), positions[None, :], queries, keys, values],
        [pltpu.VMEM((384, 8), F32)],
        smem=(0,),
    )
    pair = (
        keep
        + seq_pp(keep, lambda i: i ^ 1)
        + seq_pp(away, lambda i: i ^ 2)
        + seq_pp(away, lambda i: i ^ 3)
    )

    line_count = head_count // 4
    side = jnp.stack([place % 2, place // 2 % 2]).astype(jnp.int32)
    cut = kernel_call(
        cut_body, shape((line_count, width, 4 * width), BF16), [out_weight, keep], hbm=(1,)
    )
    pair, first_kv, last_kv, cut = lax.optimization_barrier((pair, first_kv, last_kv, cut))
    before = seq_pp(last_kv, lambda i: i + 1)
    after = seq_pp(first_kv, lambda i: i - 1)
    weights = lax.all_to_all(
        cut,
        "head",
        0,
        0,
        axis_index_groups=[[4 * x + k for x in range(line_count)] for k in range(4)],
        tiled=True,
    )

    up = lambda x: seq_pp(x, lambda i: i + 2)
    down = lambda x: seq_pp(x, lambda i: i - 2)
    a1, b1 = up(pair), down(pair)
    a2, b2 = up(a1), down(b1)
    a2, b2, before, after = lax.optimization_barrier((a2, b2, before, after))

    offsets = jnp.arange(3, dtype=jnp.int32) - 1
    my_block = rank * blocks + jnp.arange(blocks, dtype=jnp.int32)
    neighbour = my_block[:, None] + offsets[None, :]
    live = (band_mask == 1) & (neighbour >= 0) & (neighbour < seq_count * blocks)
    relative = (positions // BLOCK)[None, :] - my_block[:, None]
    hits = (relative[:, None, :] == offsets[None, :, None]) & live[:, :, None]
    bias = jnp.where(jnp.any(hits, axis=1), jnp.float32(NEG), jnp.float32(0.0))[:, None, :]
    acc, stat = kernel_call(
        functools.partial(band_body, factor),
        [shape((rows, width), F32), shape((rows, HEAD_DIM), F32)],
        [live.astype(jnp.int32), queries, keys, values, before, after],
        [pltpu.VMEM((rows + 2 * BLOCK, width), BF16), pltpu.VMEM((rows + 2 * BLOCK, 2 * width), BF16)],
        smem=(0,),
    )
    a3, b3 = up(a2), down(b2)
    a3, b3, acc, stat = lax.optimization_barrier((a3, b3, acc, stat))

    half = SLOTS // 2
    a4, b4 = up(a3[:half]), down(b3[half:])
    a4, b4, weights = lax.optimization_barrier((a4, b4, weights))
    pieces = [pair, a1, b1, a2, b2, a3, b3, a4, b4]
    line = (rank // 2 + jnp.array([0, -1, 1, -2, 2, -3, 3, -4, -4], jnp.int32)) % (seq_count // 2)
    extra = jnp.array([0] * 8 + [half], jnp.int32)
    places = jnp.take(starts, line // 2) + SLOTS * (line % 2) + extra

    partial, global_keys, global_values = kernel_call(
        functools.partial(gather_body, factor, len(pieces)),
        [
            shape((total, width + CODE), BF16),
            shape((total, width), BF16),
            shape((total, width), BF16),
        ],
        [places, keys, values] + pieces,
        [
            pltpu.VMEM((total + 2 * SLOTS + 8, 3 * width), F32),
            pltpu.VMEM((total, width), BF16),
            pltpu.VMEM((rows, 2 * width), BF16),
        ],
        smem=(0,),
    )
    sent = lax.all_to_all(
        partial.reshape(seq_count, home_rows, width + CODE), "seq", 0, 0, tiled=True
    )
    attended = kernel_call(
        functools.partial(main_body, factor),
        shape((rows, width), BF16),
        [queries, bias, acc, stat, global_keys, global_values, partial],
        [pltpu.VMEM((total, 2 * width), BF16)],
        hbm=(6,),
    )

    xu = lambda x: head_pp(x, lambda i: i + 4)
    xd = lambda x: head_pp(x, lambda i: i - 4)
    mid = rows // 2
    u1, d1 = xu(attended), xd(attended)
    u2, d2 = xu(u1[:mid]), xd(d1[mid:])
    own = kernel_call(merge_body, shape((home_rows, width), BF16), [sent])
    far = [head_pp(own, lambda i: i + 4 * d) for d in range(1, line_count)]

    parts = [attended, u1, d1, u2, d2, own, *far]
    layout = [(0, 0), (0, 1), (0, 3), (0, 2), (mid, 2), (rows, 0), (rows, 1), (rows, 2), (rows, 3)]
    order = ((place // 4 - jnp.arange(line_count)) % line_count).astype(jnp.int32)
    full = shape((rows + home_rows, width), F32)

    def project(flip, parts):
        return kernel_call(
            functools.partial(project_body, layout, flip),
            [full, full],
            [side, order, *parts, weights],
            [
                pltpu.VMEM((rows + home_rows, line_count * width), BF16),
                pltpu.VMEM((line_count * width, 2 * width), BF16),
                pltpu.SemaphoreType.DMA((line_count + len(layout),)),
            ],
            smem=(0, 1),
            hbm=range(2, 3 + len(layout)),
        )

    mine, other = project(1, parts)
    other = head_pp(other, lambda i: i ^ 1)
    across = kernel_call(join_body, shape((rows + home_rows, width), BF16), [mine, other])
    mine, other = project(0, parts)
    other = head_pp(other, lambda i: i ^ 1)
    across = head_pp(across, lambda i: i ^ 2)
    return mine, other, across


def per_device(queries, keys, values, out_weight, band_mask, positions):
    rows, width = queries.shape
    seq_count = lax.axis_size("seq")
    edges = jnp.arange(seq_count // GROUP + 1, dtype=jnp.int32) * (GROUP * rows)
    starts = jnp.sum((positions[None, :] < edges[:, None]).astype(jnp.int32), axis=1, dtype=jnp.int32)
    fits = jnp.max(starts[1:] - starts[:-1]) <= 2 * SLOTS
    args = (queries, keys, values, out_weight, band_mask, positions, starts)
    home_rows = positions.shape[0] // seq_count
    slow = lax.cond(
        fits,
        lambda *_: (jnp.zeros((rows, width), BF16), jnp.zeros((home_rows, width), BF16)),
        general,
        *args,
    )
    fast = balanced(*args)
    shape = jax.ShapeDtypeStruct
    return tuple(
        kernel_call(
            final_body,
            [shape((rows, width), BF16), shape((home_rows, width), BF16)],
            [fits[None].astype(jnp.int32), *fast, *slow],
            smem=(0,),
            hbm=(4, 5),
        )
    )


def solution(mesh):
    in_specs = (
        P("seq", "head"),
        P("seq", "head"),
        P("seq", "head"),
        P("head", None),
        P("seq", None),
        P(),
    )
    out_specs = (P("seq", "head"), P("seq", "head"))
    return jax.shard_map(
        per_device, mesh=mesh, in_specs=in_specs, out_specs=out_specs, check_vma=False
    )
```

```python
import functools
import math

import jax
import jax.numpy as jnp
from jax import lax
from jax.experimental import pallas as pl
from jax.experimental.pallas import tpu as pltpu
from jax.sharding import PartitionSpec as P

HEAD_DIM = 128
BLOCK = 512
NEG = -1e30
F32 = jnp.float32
BF16 = jnp.bfloat16
VMEM = pl.BlockSpec(memory_space=pltpu.VMEM)
SMEM = pl.BlockSpec(memory_space=pltpu.SMEM)
HBM = pl.BlockSpec(memory_space=pl.ANY)
PARAMS = pltpu.CompilerParams(vmem_limit_bytes=20 * 1024 * 1024)


def kernel_call(body, outs, ins, scratch=(), smem=(), hbm=(), load=()):
    load = tuple(load)
    free = [SMEM if i in smem else HBM if i in hbm or i in load else VMEM for i in range(len(ins))]
    held = [pltpu.VMEM(ins[i].shape, ins[i].dtype) for i in load]
    sems = [pltpu.SemaphoreType.DMA((len(load),))] if load else []

    def run(*refs):
        refs = list(refs)
        if load:
            copies = []
            for n, i in enumerate(load):
                to = refs[len(refs) - len(load) - 1 + n]
                copies.append(pltpu.make_async_copy(refs[i], to, refs[-1].at[n]))
                refs[i] = to
            for copy in copies:
                copy.start()
            for copy in copies:
                copy.wait()
            refs = refs[: len(refs) - len(load) - 1]
        body(*refs)

    return pl.pallas_call(
        run,
        out_shape=outs,
        in_specs=free,
        out_specs=jax.tree.map(lambda _: VMEM, outs),
        scratch_shapes=[*scratch, *held, *sems],
        compiler_params=PARAMS,
    )(*ins)


def dot_nt(a, b):
    return lax.dot_general(a, b, (((1,), (1,)), ((), ())), preferred_element_type=F32)


def dot_nn(a, b):
    return lax.dot_general(a, b, (((1,), (0,)), ((), ())), preferred_element_type=F32)


def extended(cells, sides, width):
    for axis, dim in sides:
        count = lax.axis_size(axis)
        ends = count - 1
        head = lax.slice_in_dim(cells, 0, width, axis=dim)
        tail = lax.slice_in_dim(cells, cells.shape[dim] - width, cells.shape[dim], axis=dim)
        cells = jnp.concatenate(
            [
                lax.ppermute(tail, axis, [(i, (i + 1) % count) for i in range(ends)]),
                cells,
                lax.ppermute(head, axis, [((i + 1) % count, i) for i in range(ends)]),
            ],
            axis=dim,
        )
    return cells


def band_block(
    query_rows, band_keys, band_values, band_live, summary_keys, summary_values, global_live, scale
):
    count = query_rows.shape[0]
    heads_here = query_rows.shape[1] // HEAD_DIM
    globals_all = summary_keys.shape[0]
    query_heads = query_rows.reshape(count, heads_here, HEAD_DIM)
    global_key_heads = summary_keys.reshape(globals_all, heads_here, HEAD_DIM)
    global_value_heads = summary_values.reshape(globals_all, heads_here, HEAD_DIM)
    global_scores = (
        jnp.einsum(
            "qhd,khd->hqk", query_heads, global_key_heads, preferred_element_type=jnp.float32
        )
        * scale
    )
    global_scores = jnp.where(global_live[None, None, :], global_scores, -jnp.inf)
    key_heads = band_keys.reshape(3 * BLOCK, heads_here, HEAD_DIM)
    value_heads = band_values.reshape(3 * BLOCK, heads_here, HEAD_DIM)
    band_scores = (
        jnp.einsum("qhd,khd->hqk", query_heads, key_heads, preferred_element_type=jnp.float32)
        * scale
    )
    band_scores = jnp.where(jnp.repeat(band_live, BLOCK)[None, None, :], band_scores, -jnp.inf)
    peak = jnp.maximum(jnp.max(band_scores, axis=-1), jnp.max(global_scores, axis=-1))
    band_weights = jnp.exp(band_scores - peak[:, :, None])
    global_weights = jnp.exp(global_scores - peak[:, :, None])
    totals = jnp.sum(band_weights, axis=-1) + jnp.sum(global_weights, axis=-1)
    band_probs = band_weights.astype(jnp.bfloat16)
    global_probs = global_weights.astype(jnp.bfloat16)
    summed = jnp.einsum(
        "hqk,khd->qhd", global_probs, global_value_heads, preferred_element_type=jnp.float32
    )
    summed = summed + jnp.einsum(
        "hqk,khd->qhd", band_probs, value_heads, preferred_element_type=jnp.float32
    )
    result = summed / jnp.transpose(totals)[:, :, None]
    return result.reshape(count, heads_here * HEAD_DIM).astype(jnp.bfloat16)


def general(queries, keys, values, out_weight, band_mask, summary_positions, starts):
    tok_rows, width = queries.shape
    heads_here = width // HEAD_DIM
    blocks_here = tok_rows // BLOCK
    seq_count = lax.axis_size("seq")
    seq_rank = lax.axis_index("seq")
    first_token = seq_rank * tok_rows
    total_blocks = seq_count * blocks_here
    globals_all = summary_positions.shape[0]
    glob_rows = globals_all // seq_count
    scale = jnp.float32(1.0 / math.sqrt(HEAD_DIM))
    local_place = summary_positions - first_token
    owned = (local_place >= 0) & (local_place < tok_rows)
    picked_index = jnp.clip(local_place, 0, tok_rows - 1)
    picked_queries = jnp.where(owned[:, None], jnp.take(queries, picked_index, axis=0), 0)
    picked_keys = jnp.where(owned[:, None], jnp.take(keys, picked_index, axis=0), 0)
    picked_values = jnp.where(owned[:, None], jnp.take(values, picked_index, axis=0), 0)
    gathered = (
        lax.psum(picked_queries, "seq").astype(jnp.float32),
        lax.psum(picked_keys, "seq").astype(jnp.float32),
        lax.psum(picked_values, "seq").astype(jnp.float32),
    )
    summary_queries = gathered[0].astype(jnp.bfloat16)
    summary_keys = gathered[1].astype(jnp.bfloat16)
    summary_values = gathered[2].astype(jnp.bfloat16)
    paired = jnp.stack([keys, values], axis=1)
    padded = extended(paired, (("seq", 0),), BLOCK)
    summary_blocks = summary_positions // BLOCK
    offsets = jnp.arange(3, dtype=jnp.int32) - 1
    outputs = []
    for block_index in range(blocks_here):
        query_rows = queries[block_index * BLOCK : (block_index + 1) * BLOCK]
        window = padded[block_index * BLOCK : block_index * BLOCK + 3 * BLOCK]
        my_block = seq_rank * blocks_here + block_index
        neighbour = my_block + offsets
        exists = (neighbour >= 0) & (neighbour < total_blocks)
        band_live = (band_mask[block_index] == 1) & exists
        relative = summary_blocks - my_block
        hits = (relative[:, None] == offsets[None, :]) & band_live[None, :]
        global_live = jnp.logical_not(jnp.any(hits, axis=1))
        outputs.append(
            band_block(
                query_rows,
                window[:, 0],
                window[:, 1],
                band_live,
                summary_keys,
                summary_values,
                global_live,
                scale,
            )
        )
    attended = jnp.concatenate(outputs, axis=0)
    key_heads = keys.reshape(tok_rows, heads_here, HEAD_DIM)
    value_heads = values.reshape(tok_rows, heads_here, HEAD_DIM)
    query_heads = summary_queries.reshape(globals_all, heads_here, HEAD_DIM)
    summary_scores = (
        jnp.einsum("ghd,khd->hgk", query_heads, key_heads, preferred_element_type=jnp.float32)
        * scale
    )
    local_peak = jnp.max(summary_scores, axis=-1)
    summary_peak = lax.pmax(local_peak, "seq")
    summary_weights = jnp.exp(summary_scores - summary_peak[:, :, None])
    part_totals = jnp.transpose(jnp.sum(summary_weights, axis=-1))
    summary_probs = summary_weights.astype(jnp.bfloat16)
    part_sums = jnp.einsum(
        "hgk,khd->ghd", summary_probs, value_heads, preferred_element_type=jnp.float32
    ).reshape(globals_all, width)
    every_sums, every_totals = lax.psum((part_sums, part_totals), "seq")
    own_sums = lax.dynamic_slice_in_dim(every_sums, seq_rank * glob_rows, glob_rows, 0)
    own_totals = lax.dynamic_slice_in_dim(every_totals, seq_rank * glob_rows, glob_rows, 0)
    summary_attended = (
        (own_sums.reshape(glob_rows, heads_here, HEAD_DIM) / own_totals[:, :, None])
        .reshape(glob_rows, width)
        .astype(jnp.bfloat16)
    )
    all_rows = jnp.concatenate([attended, summary_attended], axis=0)
    features = jnp.transpose(
        lax.psum_scatter(
            lax.dot_general(
                out_weight, all_rows, (((0,), (1,)), ((), ())), preferred_element_type=jnp.float32
            ),
            "head",
            scatter_dimension=0,
            tiled=True,
        )
    )
    result = features.astype(jnp.bfloat16)
    return (result[:tok_rows], result[tok_rows:])


GROUP = 4
SLOTS = 160
CODE = 128


def edge_body(k, v, turn, first_kv, last_kv):
    rows, width = k.shape
    first_kv[:, :width] = k[:BLOCK, :]
    first_kv[:, width:] = v[:BLOCK, :]
    last_kv[:, :width] = k[rows - BLOCK :, :]
    last_kv[:, width:] = v[rows - BLOCK :, :]


def cut_body(w, after, out):
    chips, _, width = out.shape
    for c in range(chips):
        out[c, :, :] = w[:, c * width : (c + 1) * width]


def pick_body(rank, positions, q, k, v, *refs):
    outs, column = refs[:2], refs[2]
    rows, width = q.shape
    me = rank[0]
    group, half = me // GROUP, (me % GROUP) // 2
    total = positions.shape[1]
    where = positions[...]
    begin = jnp.sum((where < group * GROUP * rows).astype(F32)).astype(jnp.int32)
    local = jnp.where(
        (where >= group * GROUP * rows) & (where < (group + 1) * GROUP * rows),
        where - me * rows,
        -1,
    )
    wide = jnp.broadcast_to(local, (8, total))
    wide = pltpu.roll(wide, lax.rem(total - begin // 16 * 16, total), 1)[:, :384]
    lane = lax.broadcasted_iota(jnp.int32, wide.shape, 1)
    wide = jnp.where(lane < 2 * SLOTS, wide, -1)
    column[...] = jnp.transpose(wide.astype(F32))
    lanes = lax.broadcasted_iota(jnp.int32, (SLOTS, rows), 1).astype(F32)
    for part in range(2):
        at = pl.multiple_of((half ^ part) * SLOTS, 8)
        hot = jnp.where(column[pl.ds(at, SLOTS), :1] == lanes, 1.0, 0.0).astype(BF16)
        for i, ref in enumerate((q, k, v)):
            rows_here = dot_nn(hot, ref[...]).astype(BF16)
            outs[part][:, i * width : (i + 1) * width] = rows_here


def band_body(factor, live, q, k, v, before, after, acc, stat, out, ke, ve):
    rows, width = q.shape
    heads = width // HEAD_DIM
    tile = 256
    window = 3 * BLOCK
    ke[:BLOCK, :] = before[:, :width]
    ke[BLOCK : BLOCK + rows, :] = k[...]
    ke[BLOCK + rows :, :] = after[:, :width]
    for h in range(heads):
        src = slice(h * HEAD_DIM, (h + 1) * HEAD_DIM)
        off = slice(width + h * HEAD_DIM, width + (h + 1) * HEAD_DIM)
        dst = slice(2 * h * HEAD_DIM, (2 * h + 1) * HEAD_DIM)
        one = slice((2 * h + 1) * HEAD_DIM, (2 * h + 2) * HEAD_DIM)
        ve[:BLOCK, dst] = before[:, off]
        ve[BLOCK : BLOCK + rows, dst] = v[:, src]
        ve[BLOCK + rows :, dst] = after[:, off]
        ve[:, one] = jnp.ones((ve.shape[0], HEAD_DIM), BF16)

    def step(t, carry):
        block = t // (BLOCK // tile)
        at = pl.multiple_of(t * tile, tile)
        base = pl.multiple_of(block * BLOCK, BLOCK)
        for h in range(heads):
            cols = slice(h * HEAD_DIM, (h + 1) * HEAD_DIM)
            qt = q[pl.ds(at, tile), cols]
            parts = []
            for j in range(3):
                s = dot_nt(qt, ke[pl.ds(base + j * BLOCK, BLOCK), cols]) * factor
                parts.append(jnp.where(live[block, j] == 1, s, NEG))
            far_sum = stat[pl.ds(at, tile), 2 * h : 2 * h + 1]
            far_peak = stat[pl.ds(at, tile), 2 * h + 1 : 2 * h + 2]
            peak = functools.reduce(
                jnp.maximum, [far_peak] + [jnp.max(s, axis=1, keepdims=True) for s in parts]
            )
            both = None
            for j in range(3):
                p = jnp.exp2(parts[j] - peak).astype(BF16)
                o = dot_nn(
                    p, ve[pl.ds(base + j * BLOCK, BLOCK), 2 * h * HEAD_DIM : (2 * h + 2) * HEAD_DIM]
                )
                both = o if both is None else both + o
            back = jnp.exp2(far_peak - peak)
            num = both[:, :HEAD_DIM] + back * acc[pl.ds(at, tile), cols]
            den = both[:, HEAD_DIM:] + back * far_sum
            out[pl.ds(at, tile), cols] = (num / den).astype(BF16)
        return carry

    lax.fori_loop(0, rows // tile, step, 0, unroll=2)


def summary_body(factor, qg, k, v, out, ve):
    rows, width = k.shape
    heads = width // HEAD_DIM
    tile = 256
    for h in range(heads):
        ve[:, 2 * h * HEAD_DIM : (2 * h + 1) * HEAD_DIM] = v[:, h * HEAD_DIM : (h + 1) * HEAD_DIM]
        ve[:, (2 * h + 1) * HEAD_DIM : (2 * h + 2) * HEAD_DIM] = jnp.ones((rows, HEAD_DIM), BF16)
    lane = lax.broadcasted_iota(jnp.int32, (tile, CODE), 1)

    def step(t, carry):
        at = pl.multiple_of(t * tile, tile)
        code = jnp.zeros((tile, CODE), F32)
        for h in range(heads):
            cols = slice(h * HEAD_DIM, (h + 1) * HEAD_DIM)
            s = dot_nt(qg[pl.ds(at, tile), cols], k[:, cols]) * factor
            peak = jnp.max(s, axis=1, keepdims=True)
            p = jnp.exp2(s - peak).astype(BF16)
            o = dot_nn(p, ve[:, 2 * h * HEAD_DIM : (2 * h + 2) * HEAD_DIM])
            den = o[:, HEAD_DIM:]
            out[pl.ds(at, tile), cols] = (o[:, :HEAD_DIM] / den).astype(BF16)
            size = peak + jnp.log2(den)
            for piece in range(3):
                part = size.astype(BF16).astype(F32)
                code = jnp.where(lane == 3 * h + piece, part, code)
                size = size - part
        out[pl.ds(at, tile), width:] = code.astype(BF16)
        return carry

    lax.fori_loop(0, out.shape[0] // tile, step, 0, unroll=2)


def gather_body(factor, pieces, places, q, bias, *refs):
    ins, (acc, stat, q_out), (qg, kg, v, vg) = refs[:pieces], refs[pieces : pieces + 3], refs[pieces + 3 :]
    rows, width = q.shape
    heads = width // HEAD_DIM
    total = vg.shape[0]
    tile = 256
    targets = (qg, kg, v)
    for ref in targets:
        ref[...] = jnp.zeros(ref.shape, BF16)
    for n, ref in enumerate(ins):
        at = pl.ds(pl.multiple_of(places[n], 16), ref.shape[0])
        for i, target in enumerate(targets):
            target[at, :] += ref[:, i * width : (i + 1) * width]
    q_out[...] = qg[:total, :]
    for h in range(heads):
        vg[:, 2 * h * HEAD_DIM : (2 * h + 1) * HEAD_DIM] = v[
            :total, h * HEAD_DIM : (h + 1) * HEAD_DIM
        ]
        vg[:, (2 * h + 1) * HEAD_DIM : (2 * h + 2) * HEAD_DIM] = jnp.ones((total, HEAD_DIM), BF16)

    def step(t, carry):
        block = t // (BLOCK // tile)
        at = pl.multiple_of(t * tile, tile)
        code = jnp.zeros((tile, HEAD_DIM), F32)
        lane = lax.broadcasted_iota(jnp.int32, code.shape, 1)
        for h in range(heads):
            cols = slice(h * HEAD_DIM, (h + 1) * HEAD_DIM)
            s = dot_nt(q[pl.ds(at, tile), cols], kg[:total, cols]) * factor
            s = s + bias[block]
            peak = jnp.max(s, axis=1, keepdims=True)
            p = jnp.exp2(s - peak).astype(BF16)
            o = dot_nn(p, vg[:, 2 * h * HEAD_DIM : (2 * h + 2) * HEAD_DIM])
            acc[pl.ds(at, tile), cols] = o[:, :HEAD_DIM]
            pair = jnp.where(lane == 2 * h, o[:, HEAD_DIM:], peak)
            code = jnp.where(lane // 2 == h, pair, code)
        stat[pl.ds(at, tile), :] = code
        return carry

    lax.fori_loop(0, rows // tile, step, 0, unroll=2)


def merge_body(sent, out):
    count, rows, full = sent.shape
    width = full - CODE
    for h in range(width // HEAD_DIM):
        cols = slice(h * HEAD_DIM, (h + 1) * HEAD_DIM)
        sizes = []
        for s in range(count):
            code = sent[s, :, width:].astype(F32)
            sizes.append(
                code[:, 3 * h : 3 * h + 1]
                + code[:, 3 * h + 1 : 3 * h + 2]
                + code[:, 3 * h + 2 : 3 * h + 3]
            )
        peak = functools.reduce(jnp.maximum, sizes)
        num = jnp.zeros((rows, HEAD_DIM), F32)
        den = jnp.zeros((rows, 1), F32)
        for s in range(count):
            w = jnp.exp2(sizes[s] - peak)
            num = num + w * sent[s, :, cols].astype(F32)
            den = den + w
        out[:, cols] = (num / den).astype(BF16)


def project_body(layout, flips, side, order, *refs):
    pieces = len(layout)
    ins, weights = refs[:pieces], refs[pieces]
    outs, (x, w, sems) = refs[pieces + 1 : -3], refs[-3:]
    rows, width = outs[0].shape
    copies = []
    for d in range(x.shape[1] // width):
        copies.append(
            pltpu.make_async_copy(
                weights.at[order[d]], w.at[pl.ds(d * width, width), :], sems.at[d]
            )
        )
    for copy in copies:
        copy.start()
    for piece, (first, at) in zip(ins, layout):
        x[first : first + piece.shape[0], at * width : (at + 1) * width] = piece[...]
    for copy in copies:
        copy.wait()
    for n, flip in enumerate(flips):
        chip = side[1] if flip == 0 else 1 - side[1]
        for m, core in enumerate((1 - side[0], side[0])):
            out = outs[2 * n + 1 - m]
            cols = pl.ds(pl.multiple_of((2 * chip + core) * width, width), width)
            for low in range(0, rows, 256):
                high = min(low + 256, rows)
                out[low:high, :] = dot_nn(x[low:high, :], w[:, cols])


def join_body(a, b, out):
    out[...] = (a[...] + b[...]).astype(BF16)


def final_body(fits, mine, other, across, s_mine, s_other, s_across, slow, s_slow, out, s_out):
    @pl.when(fits[0] == 1)
    def _():
        out[...] = (mine[...] + other[...] + across[...].astype(F32)).astype(BF16)
        s_out[...] = (s_mine[...] + s_other[...] + s_across[...].astype(F32)).astype(BF16)

    @pl.when(fits[0] != 1)
    def _():
        pltpu.sync_copy(slow, out)
        pltpu.sync_copy(s_slow, s_out)


def balanced(slow, queries, keys, values, out_weight, band_mask, positions, starts):
    rows, width = queries.shape
    seq_count = lax.axis_size("seq")
    head_count = lax.axis_size("head")
    rank = lax.axis_index("seq")
    place = lax.axis_index("head")
    blocks = rows // BLOCK
    total = positions.shape[0]
    home_rows = total // seq_count
    factor = (1.0 / math.sqrt(HEAD_DIM)) * math.log2(math.e)
    shape = jax.ShapeDtypeStruct

    def seq_pp(x, f):
        return lax.ppermute(x, "seq", [(i, f(i) % seq_count) for i in range(seq_count)])

    def head_pp(x, f):
        return lax.ppermute(x, "head", [(i, f(i) % head_count) for i in range(head_count)])

    edge = shape((BLOCK, 2 * width), BF16)

    pick = shape((SLOTS, 3 * width), BF16)
    keep, away = kernel_call(
        pick_body,
        [pick, pick],
        [rank[None].astype(jnp.int32), positions[None, :], queries, keys, values],
        [pltpu.VMEM((384, 8), F32)],
        smem=(0,),
    )
    first_kv, last_kv = kernel_call(edge_body, [edge, edge], [keys, values, keep], hbm=(2,))
    near = seq_pp(keep, lambda i: i ^ 1)

    line_count = head_count // 4
    side = jnp.stack([place % 2, place // 2 % 2]).astype(jnp.int32)
    cut = kernel_call(
        cut_body, shape((line_count, width, 4 * width), BF16), [out_weight, first_kv], hbm=(1,)
    )
    near, cut = lax.optimization_barrier((near, cut))
    pair = keep + near + seq_pp(away, lambda i: i ^ 2) + seq_pp(away, lambda i: i ^ 3)
    weights = lax.all_to_all(
        cut,
        "head",
        0,
        0,
        axis_index_groups=[[4 * x + k for x in range(line_count)] for k in range(4)],
        tiled=True,
    )

    up = lambda x: seq_pp(x, lambda i: i + 2)
    down = lambda x: seq_pp(x, lambda i: i - 2)
    a1, b1 = up(pair), down(pair)
    a2, b2 = up(a1), down(b1)
    a2, b2, first_kv, last_kv = lax.optimization_barrier((a2, b2, first_kv, last_kv))
    before = seq_pp(last_kv, lambda i: i + 1)
    after = seq_pp(first_kv, lambda i: i - 1)
    a3, b3 = up(a2), down(b2)
    half = SLOTS // 2
    a4, b4 = up(a3[:half]), down(b3[half:])
    a4, b4, weights = lax.optimization_barrier((a4, b4, weights))
    pieces = [pair, a1, b1, a2, b2, a3, b3, a4, b4]
    line = (rank // 2 + jnp.array([0, -1, 1, -2, 2, -3, 3, -4, -4], jnp.int32)) % (seq_count // 2)
    extra = jnp.array([0] * 8 + [half], jnp.int32)
    places = jnp.take(starts // 16 * 16, line // 2) + SLOTS * (line % 2) + extra

    offsets = jnp.arange(3, dtype=jnp.int32) - 1
    my_block = rank * blocks + jnp.arange(blocks, dtype=jnp.int32)
    neighbour = my_block[:, None] + offsets[None, :]
    live = (band_mask == 1) & (neighbour >= 0) & (neighbour < seq_count * blocks)
    relative = (positions // BLOCK)[None, :] - my_block[:, None]
    hits = (relative[:, None, :] == offsets[None, :, None]) & live[:, :, None]
    bias = jnp.where(jnp.any(hits, axis=1), jnp.float32(NEG), jnp.float32(0.0))[:, None, :]
    acc, stat, summary_queries = kernel_call(
        functools.partial(gather_body, factor, len(pieces)),
        [
            shape((rows, width), F32),
            shape((rows, HEAD_DIM), F32),
            shape((total, width), BF16),
        ],
        [places, queries, bias] + pieces,
        [
            pltpu.VMEM((total + 2 * SLOTS, width), BF16),
            pltpu.VMEM((total + 2 * SLOTS, width), BF16),
            pltpu.VMEM((total + 2 * SLOTS, width), BF16),
            pltpu.VMEM((total, 2 * width), BF16),
        ],
        smem=(0,),
        load=(1,),
    )
    attended = kernel_call(
        functools.partial(band_body, factor),
        shape((rows, width), BF16),
        [live.astype(jnp.int32), queries, keys, values, before, after, acc, stat],
        [pltpu.VMEM((rows + 2 * BLOCK, width), BF16), pltpu.VMEM((rows + 2 * BLOCK, 2 * width), BF16)],
        smem=(0,),
        load=(1, 2, 3),
    )

    xu = lambda x: head_pp(x, lambda i: i + 4)
    xd = lambda x: head_pp(x, lambda i: i - 4)
    mid = rows // 2
    u1, d1 = xu(attended), xd(attended)

    partial = kernel_call(
        functools.partial(summary_body, factor),
        shape((total, width + CODE), BF16),
        [summary_queries, keys, values],
        [pltpu.VMEM((rows, 2 * width), BF16)],
        load=(1, 2),
    )
    sent = lax.all_to_all(
        partial.reshape(seq_count, home_rows, width + CODE), "seq", 0, 0, tiled=True
    )
    u2, d2 = xu(u1[:mid]), xd(d1[mid:])
    order = ((place // 4 - jnp.arange(line_count)) % line_count).astype(jnp.int32)

    def project(layout, flips, parts, count):
        full = shape((count, width), F32)
        return kernel_call(
            functools.partial(project_body, layout, flips),
            [full] * (2 * len(flips)),
            [side, order, *parts, weights],
            [
                pltpu.VMEM((count, line_count * width), BF16),
                pltpu.VMEM((line_count * width, 4 * width), BF16),
                pltpu.SemaphoreType.DMA((line_count,)),
            ],
            smem=(0, 1),
            hbm=(2 + len(layout),),
        )

    layout = [(0, 0), (0, 1), (0, 3), (0, 2), (mid, 2)]
    parts = [attended, u1, d1, u2, d2]
    mine, other = project(layout, (1,), parts, rows)
    other = head_pp(other, lambda i: i ^ 1)
    across = kernel_call(join_body, shape((rows, width), BF16), [mine, other])
    across, sent = lax.optimization_barrier((across, sent))
    across = head_pp(across, lambda i: i ^ 2)
    mine, other = project(layout, (0,), parts, rows)
    other = head_pp(other, lambda i: i ^ 1)

    own = kernel_call(merge_body, shape((home_rows, width), BF16), [sent])
    far = [head_pp(own, lambda i: i + 4 * d) for d in range(1, line_count)]
    s_layout = [(0, d) for d in range(line_count)]
    s_sums = project(s_layout, (1, 0), [own, *far], home_rows)
    s_other = head_pp(jnp.concatenate([s_sums[1], s_sums[3]], axis=0), lambda i: i ^ 1)
    s_other, across = lax.optimization_barrier((s_other, across))
    s_across = kernel_call(
        join_body, shape((home_rows, width), BF16), [s_sums[0], s_other[:home_rows]]
    )
    s_across = head_pp(s_across, lambda i: i ^ 2)
    return mine, other, across, s_sums[2], s_other[home_rows:], s_across, *slow


def per_device(queries, keys, values, out_weight, band_mask, positions):
    rows, width = queries.shape
    seq_count = lax.axis_size("seq")
    edges = jnp.arange(seq_count // GROUP + 1, dtype=jnp.int32) * (GROUP * rows)
    starts = jnp.sum((positions[None, :] < edges[:, None]).astype(jnp.int32), axis=1, dtype=jnp.int32)
    fits = jnp.max(starts[1:] - starts[:-1] // 16 * 16) <= 2 * SLOTS
    args = (queries, keys, values, out_weight, band_mask, positions, starts)
    home_rows = positions.shape[0] // seq_count
    slow = lax.cond(
        fits,
        lambda *_: (jnp.zeros((rows, width), BF16), jnp.zeros((home_rows, width), BF16)),
        general,
        *args,
    )
    parts = balanced(slow, *args)
    shape = jax.ShapeDtypeStruct
    return tuple(
        kernel_call(
            final_body,
            [shape((rows, width), BF16), shape((home_rows, width), BF16)],
            [fits[None].astype(jnp.int32), *parts],
            smem=(0,),
            hbm=(7, 8),
        )
    )


def solution(mesh):
    in_specs = (
        P("seq", "head"),
        P("seq", "head"),
        P("seq", "head"),
        P("head", None),
        P("seq", None),
        P(),
    )
    out_specs = (P("seq", "head"), P("seq", "head"))
    return jax.shard_map(
        per_device, mesh=mesh, in_specs=in_specs, out_specs=out_specs, check_vma=False
    )
```

```python
import functools
import math

import jax
import jax.numpy as jnp
from jax import lax
from jax.experimental import pallas as pl
from jax.experimental.pallas import tpu as pltpu
from jax.sharding import PartitionSpec as P

HEAD_DIM = 128
BLOCK = 512
NEG = -1e30
F32 = jnp.float32
BF16 = jnp.bfloat16
VMEM = pl.BlockSpec(memory_space=pltpu.VMEM)
SMEM = pl.BlockSpec(memory_space=pltpu.SMEM)
HBM = pl.BlockSpec(memory_space=pl.ANY)
PARAMS = pltpu.CompilerParams(vmem_limit_bytes=14 * 1024 * 1024)


def kernel_call(body, outs, ins, scratch=(), smem=(), hbm=(), load=()):
    load = tuple(load)
    free = [SMEM if i in smem else HBM if i in hbm or i in load else VMEM for i in range(len(ins))]
    held = [pltpu.VMEM(ins[i].shape, ins[i].dtype) for i in load]
    sems = [pltpu.SemaphoreType.DMA((len(load),))] if load else []

    def run(*refs):
        refs = list(refs)
        if load:
            copies = []
            for n, i in enumerate(load):
                to = refs[len(refs) - len(load) - 1 + n]
                copies.append(pltpu.make_async_copy(refs[i], to, refs[-1].at[n]))
                refs[i] = to
            for copy in copies:
                copy.start()
            for copy in copies:
                copy.wait()
            refs = refs[: len(refs) - len(load) - 1]
        body(*refs)

    return pl.pallas_call(
        run,
        out_shape=outs,
        in_specs=free,
        out_specs=jax.tree.map(lambda _: VMEM, outs),
        scratch_shapes=[*scratch, *held, *sems],
        compiler_params=PARAMS,
    )(*ins)


def dot_nt(a, b):
    return lax.dot_general(a, b, (((1,), (1,)), ((), ())), preferred_element_type=F32)


def dot_nn(a, b):
    return lax.dot_general(a, b, (((1,), (0,)), ((), ())), preferred_element_type=F32)


def extended(cells, sides, width):
    for axis, dim in sides:
        count = lax.axis_size(axis)
        ends = count - 1
        head = lax.slice_in_dim(cells, 0, width, axis=dim)
        tail = lax.slice_in_dim(cells, cells.shape[dim] - width, cells.shape[dim], axis=dim)
        cells = jnp.concatenate(
            [
                lax.ppermute(tail, axis, [(i, (i + 1) % count) for i in range(ends)]),
                cells,
                lax.ppermute(head, axis, [((i + 1) % count, i) for i in range(ends)]),
            ],
            axis=dim,
        )
    return cells


def band_block(
    query_rows, band_keys, band_values, band_live, summary_keys, summary_values, global_live, scale
):
    count = query_rows.shape[0]
    heads_here = query_rows.shape[1] // HEAD_DIM
    globals_all = summary_keys.shape[0]
    query_heads = query_rows.reshape(count, heads_here, HEAD_DIM)
    global_key_heads = summary_keys.reshape(globals_all, heads_here, HEAD_DIM)
    global_value_heads = summary_values.reshape(globals_all, heads_here, HEAD_DIM)
    global_scores = (
        jnp.einsum(
            "qhd,khd->hqk", query_heads, global_key_heads, preferred_element_type=jnp.float32
        )
        * scale
    )
    global_scores = jnp.where(global_live[None, None, :], global_scores, -jnp.inf)
    key_heads = band_keys.reshape(3 * BLOCK, heads_here, HEAD_DIM)
    value_heads = band_values.reshape(3 * BLOCK, heads_here, HEAD_DIM)
    band_scores = (
        jnp.einsum("qhd,khd->hqk", query_heads, key_heads, preferred_element_type=jnp.float32)
        * scale
    )
    band_scores = jnp.where(jnp.repeat(band_live, BLOCK)[None, None, :], band_scores, -jnp.inf)
    peak = jnp.maximum(jnp.max(band_scores, axis=-1), jnp.max(global_scores, axis=-1))
    band_weights = jnp.exp(band_scores - peak[:, :, None])
    global_weights = jnp.exp(global_scores - peak[:, :, None])
    totals = jnp.sum(band_weights, axis=-1) + jnp.sum(global_weights, axis=-1)
    band_probs = band_weights.astype(jnp.bfloat16)
    global_probs = global_weights.astype(jnp.bfloat16)
    summed = jnp.einsum(
        "hqk,khd->qhd", global_probs, global_value_heads, preferred_element_type=jnp.float32
    )
    summed = summed + jnp.einsum(
        "hqk,khd->qhd", band_probs, value_heads, preferred_element_type=jnp.float32
    )
    result = summed / jnp.transpose(totals)[:, :, None]
    return result.reshape(count, heads_here * HEAD_DIM).astype(jnp.bfloat16)


def general(queries, keys, values, out_weight, band_mask, summary_positions, starts):
    tok_rows, width = queries.shape
    heads_here = width // HEAD_DIM
    blocks_here = tok_rows // BLOCK
    seq_count = lax.axis_size("seq")
    seq_rank = lax.axis_index("seq")
    first_token = seq_rank * tok_rows
    total_blocks = seq_count * blocks_here
    globals_all = summary_positions.shape[0]
    glob_rows = globals_all // seq_count
    scale = jnp.float32(1.0 / math.sqrt(HEAD_DIM))
    local_place = summary_positions - first_token
    owned = (local_place >= 0) & (local_place < tok_rows)
    picked_index = jnp.clip(local_place, 0, tok_rows - 1)
    picked_queries = jnp.where(owned[:, None], jnp.take(queries, picked_index, axis=0), 0)
    picked_keys = jnp.where(owned[:, None], jnp.take(keys, picked_index, axis=0), 0)
    picked_values = jnp.where(owned[:, None], jnp.take(values, picked_index, axis=0), 0)
    gathered = (
        lax.psum(picked_queries, "seq").astype(jnp.float32),
        lax.psum(picked_keys, "seq").astype(jnp.float32),
        lax.psum(picked_values, "seq").astype(jnp.float32),
    )
    summary_queries = gathered[0].astype(jnp.bfloat16)
    summary_keys = gathered[1].astype(jnp.bfloat16)
    summary_values = gathered[2].astype(jnp.bfloat16)
    paired = jnp.stack([keys, values], axis=1)
    padded = extended(paired, (("seq", 0),), BLOCK)
    summary_blocks = summary_positions // BLOCK
    offsets = jnp.arange(3, dtype=jnp.int32) - 1
    outputs = []
    for block_index in range(blocks_here):
        query_rows = queries[block_index * BLOCK : (block_index + 1) * BLOCK]
        window = padded[block_index * BLOCK : block_index * BLOCK + 3 * BLOCK]
        my_block = seq_rank * blocks_here + block_index
        neighbour = my_block + offsets
        exists = (neighbour >= 0) & (neighbour < total_blocks)
        band_live = (band_mask[block_index] == 1) & exists
        relative = summary_blocks - my_block
        hits = (relative[:, None] == offsets[None, :]) & band_live[None, :]
        global_live = jnp.logical_not(jnp.any(hits, axis=1))
        outputs.append(
            band_block(
                query_rows,
                window[:, 0],
                window[:, 1],
                band_live,
                summary_keys,
                summary_values,
                global_live,
                scale,
            )
        )
    attended = jnp.concatenate(outputs, axis=0)
    key_heads = keys.reshape(tok_rows, heads_here, HEAD_DIM)
    value_heads = values.reshape(tok_rows, heads_here, HEAD_DIM)
    query_heads = summary_queries.reshape(globals_all, heads_here, HEAD_DIM)
    summary_scores = (
        jnp.einsum("ghd,khd->hgk", query_heads, key_heads, preferred_element_type=jnp.float32)
        * scale
    )
    local_peak = jnp.max(summary_scores, axis=-1)
    summary_peak = lax.pmax(local_peak, "seq")
    summary_weights = jnp.exp(summary_scores - summary_peak[:, :, None])
    part_totals = jnp.transpose(jnp.sum(summary_weights, axis=-1))
    summary_probs = summary_weights.astype(jnp.bfloat16)
    part_sums = jnp.einsum(
        "hgk,khd->ghd", summary_probs, value_heads, preferred_element_type=jnp.float32
    ).reshape(globals_all, width)
    every_sums, every_totals = lax.psum((part_sums, part_totals), "seq")
    own_sums = lax.dynamic_slice_in_dim(every_sums, seq_rank * glob_rows, glob_rows, 0)
    own_totals = lax.dynamic_slice_in_dim(every_totals, seq_rank * glob_rows, glob_rows, 0)
    summary_attended = (
        (own_sums.reshape(glob_rows, heads_here, HEAD_DIM) / own_totals[:, :, None])
        .reshape(glob_rows, width)
        .astype(jnp.bfloat16)
    )
    all_rows = jnp.concatenate([attended, summary_attended], axis=0)
    features = jnp.transpose(
        lax.psum_scatter(
            lax.dot_general(
                out_weight, all_rows, (((0,), (1,)), ((), ())), preferred_element_type=jnp.float32
            ),
            "head",
            scatter_dimension=0,
            tiled=True,
        )
    )
    result = features.astype(jnp.bfloat16)
    return (result[:tok_rows], result[tok_rows:])


GROUP = 4
SLOTS = 160
CODE = 128


def edge_body(k, v, turn, first_kv, last_kv):
    rows, width = k.shape
    first_kv[:, :width] = k[:BLOCK, :]
    first_kv[:, width:] = v[:BLOCK, :]
    last_kv[:, :width] = k[rows - BLOCK :, :]
    last_kv[:, width:] = v[rows - BLOCK :, :]


def cut_body(w, after, out):
    chips, _, width = out.shape
    for c in range(chips):
        out[c, :, :] = w[:, c * width : (c + 1) * width]


def pick_body(rank, positions, q, k, v, *refs):
    outs, column = refs[:2], refs[2]
    rows, width = q.shape
    me = rank[0]
    group, half = me // GROUP, (me % GROUP) // 2
    total = positions.shape[1]
    where = positions[...]
    begin = jnp.sum((where < group * GROUP * rows).astype(F32)).astype(jnp.int32)
    local = jnp.where(
        (where >= group * GROUP * rows) & (where < (group + 1) * GROUP * rows),
        where - me * rows,
        -1,
    )
    wide = jnp.broadcast_to(local, (8, total))
    wide = pltpu.roll(wide, lax.rem(total - begin // 16 * 16, total), 1)[:, :384]
    lane = lax.broadcasted_iota(jnp.int32, wide.shape, 1)
    wide = jnp.where(lane < 2 * SLOTS, wide, -1)
    column[...] = jnp.transpose(wide.astype(F32))
    lanes = lax.broadcasted_iota(jnp.int32, (SLOTS, rows), 1).astype(F32)
    for part in range(2):
        at = pl.multiple_of((half ^ part) * SLOTS, 8)
        hot = jnp.where(column[pl.ds(at, SLOTS), :1] == lanes, 1.0, 0.0).astype(BF16)
        for i, ref in enumerate((q, k, v)):
            rows_here = dot_nn(hot, ref[...]).astype(BF16)
            outs[part][:, i * width : (i + 1) * width] = rows_here


def band_body(factor, live, q, k, v, before, after, acc, stat, out, ke, ve):
    rows, width = q.shape
    heads = width // HEAD_DIM
    tile = 256
    window = 3 * BLOCK
    ke[:BLOCK, :] = before[:, :width]
    ke[BLOCK : BLOCK + rows, :] = k[...]
    ke[BLOCK + rows :, :] = after[:, :width]
    for h in range(heads):
        src = slice(h * HEAD_DIM, (h + 1) * HEAD_DIM)
        off = slice(width + h * HEAD_DIM, width + (h + 1) * HEAD_DIM)
        dst = slice(2 * h * HEAD_DIM, (2 * h + 1) * HEAD_DIM)
        one = slice((2 * h + 1) * HEAD_DIM, (2 * h + 2) * HEAD_DIM)
        ve[:BLOCK, dst] = before[:, off]
        ve[BLOCK : BLOCK + rows, dst] = v[:, src]
        ve[BLOCK + rows :, dst] = after[:, off]
        ve[:, one] = jnp.ones((ve.shape[0], HEAD_DIM), BF16)

    def step(t, carry):
        block = t // (BLOCK // tile)
        at = pl.multiple_of(t * tile, tile)
        base = pl.multiple_of(block * BLOCK, BLOCK)
        for h in range(heads):
            cols = slice(h * HEAD_DIM, (h + 1) * HEAD_DIM)
            qt = q[pl.ds(at, tile), cols]
            parts = []
            for j in range(3):
                s = dot_nt(qt, ke[pl.ds(base + j * BLOCK, BLOCK), cols]) * factor
                parts.append(jnp.where(live[block, j] == 1, s, NEG))
            far_sum = stat[pl.ds(at, tile), 2 * h : 2 * h + 1]
            far_peak = stat[pl.ds(at, tile), 2 * h + 1 : 2 * h + 2]
            peak = functools.reduce(
                jnp.maximum, [far_peak] + [jnp.max(s, axis=1, keepdims=True) for s in parts]
            )
            both = None
            for j in range(3):
                p = jnp.exp2(parts[j] - peak).astype(BF16)
                o = dot_nn(
                    p, ve[pl.ds(base + j * BLOCK, BLOCK), 2 * h * HEAD_DIM : (2 * h + 2) * HEAD_DIM]
                )
                both = o if both is None else both + o
            back = jnp.exp2(far_peak - peak)
            num = both[:, :HEAD_DIM] + back * acc[pl.ds(at, tile), cols]
            den = both[:, HEAD_DIM:] + back * far_sum
            out[pl.ds(at, tile), cols] = (num / den).astype(BF16)
        return carry

    lax.fori_loop(0, rows // tile, step, 0, unroll=2)


def summary_body(factor, qg, k, v, out, ve):
    rows, width = k.shape
    heads = width // HEAD_DIM
    tile = 256
    for h in range(heads):
        ve[:, 2 * h * HEAD_DIM : (2 * h + 1) * HEAD_DIM] = v[:, h * HEAD_DIM : (h + 1) * HEAD_DIM]
        ve[:, (2 * h + 1) * HEAD_DIM : (2 * h + 2) * HEAD_DIM] = jnp.ones((rows, HEAD_DIM), BF16)
    lane = lax.broadcasted_iota(jnp.int32, (tile, CODE), 1)

    def step(t, carry):
        at = pl.multiple_of(t * tile, tile)
        code = jnp.zeros((tile, CODE), F32)
        for h in range(heads):
            cols = slice(h * HEAD_DIM, (h + 1) * HEAD_DIM)
            s = dot_nt(qg[pl.ds(at, tile), cols], k[:, cols]) * factor
            peak = jnp.max(s, axis=1, keepdims=True)
            p = jnp.exp2(s - peak).astype(BF16)
            o = dot_nn(p, ve[:, 2 * h * HEAD_DIM : (2 * h + 2) * HEAD_DIM])
            den = o[:, HEAD_DIM:]
            out[pl.ds(at, tile), cols] = (o[:, :HEAD_DIM] / den).astype(BF16)
            size = peak + jnp.log2(den)
            for piece in range(3):
                part = size.astype(BF16).astype(F32)
                code = jnp.where(lane == 3 * h + piece, part, code)
                size = size - part
        out[pl.ds(at, tile), width:] = code.astype(BF16)
        return carry

    lax.fori_loop(0, out.shape[0] // tile, step, 0, unroll=2)


def gather_body(factor, pieces, places, q, bias, *refs):
    ins, (acc, stat, q_out), (qg, kg, v, vg) = refs[:pieces], refs[pieces : pieces + 3], refs[pieces + 3 :]
    rows, width = q.shape
    heads = width // HEAD_DIM
    total = vg.shape[0]
    tile = 256
    targets = (qg, kg, v)
    for ref in targets:
        ref[...] = jnp.zeros(ref.shape, BF16)
    for n, ref in enumerate(ins):
        at = pl.ds(pl.multiple_of(places[n], 16), ref.shape[0])
        for i, target in enumerate(targets):
            target[at, :] += ref[:, i * width : (i + 1) * width]
    q_out[...] = qg[:total, :]
    for h in range(heads):
        vg[:, 2 * h * HEAD_DIM : (2 * h + 1) * HEAD_DIM] = v[
            :total, h * HEAD_DIM : (h + 1) * HEAD_DIM
        ]
        vg[:, (2 * h + 1) * HEAD_DIM : (2 * h + 2) * HEAD_DIM] = jnp.ones((total, HEAD_DIM), BF16)

    def step(t, carry):
        block = t // (BLOCK // tile)
        at = pl.multiple_of(t * tile, tile)
        code = jnp.zeros((tile, HEAD_DIM), F32)
        lane = lax.broadcasted_iota(jnp.int32, code.shape, 1)
        for h in range(heads):
            cols = slice(h * HEAD_DIM, (h + 1) * HEAD_DIM)
            s = dot_nt(q[pl.ds(at, tile), cols], kg[:total, cols]) * factor
            s = s + bias[block]
            peak = jnp.max(s, axis=1, keepdims=True)
            p = jnp.exp2(s - peak).astype(BF16)
            o = dot_nn(p, vg[:, 2 * h * HEAD_DIM : (2 * h + 2) * HEAD_DIM])
            acc[pl.ds(at, tile), cols] = o[:, :HEAD_DIM]
            pair = jnp.where(lane == 2 * h, o[:, HEAD_DIM:], peak)
            code = jnp.where(lane // 2 == h, pair, code)
        stat[pl.ds(at, tile), :] = code
        return carry

    lax.fori_loop(0, rows // tile, step, 0, unroll=2)


def merge_body(sent, out):
    count, rows, full = sent.shape
    width = full - CODE
    for h in range(width // HEAD_DIM):
        cols = slice(h * HEAD_DIM, (h + 1) * HEAD_DIM)
        sizes = []
        for s in range(count):
            code = sent[s, :, width:].astype(F32)
            sizes.append(
                code[:, 3 * h : 3 * h + 1]
                + code[:, 3 * h + 1 : 3 * h + 2]
                + code[:, 3 * h + 2 : 3 * h + 3]
            )
        peak = functools.reduce(jnp.maximum, sizes)
        num = jnp.zeros((rows, HEAD_DIM), F32)
        den = jnp.zeros((rows, 1), F32)
        for s in range(count):
            w = jnp.exp2(sizes[s] - peak)
            num = num + w * sent[s, :, cols].astype(F32)
            den = den + w
        out[:, cols] = (num / den).astype(BF16)


def project_body(layout, flips, side, order, *refs):
    pieces = len(layout)
    ins, weights = refs[:pieces], refs[pieces]
    outs, (x, w, sems) = refs[pieces + 1 : -3], refs[-3:]
    rows, width = outs[0].shape
    copies = []
    for d in range(x.shape[1] // width):
        copies.append(
            pltpu.make_async_copy(
                weights.at[order[d]], w.at[pl.ds(d * width, width), :], sems.at[d]
            )
        )
    for copy in copies:
        copy.start()
    for piece, (first, at) in zip(ins, layout):
        x[first : first + piece.shape[0], at * width : (at + 1) * width] = piece[...]
    for copy in copies:
        copy.wait()
    for n, flip in enumerate(flips):
        chip = side[1] if flip == 0 else 1 - side[1]
        for m, core in enumerate((1 - side[0], side[0])):
            out = outs[2 * n + 1 - m]
            cols = pl.ds(pl.multiple_of((2 * chip + core) * width, width), width)
            for low in range(0, rows, 256):
                high = min(low + 256, rows)
                out[low:high, :] = dot_nn(x[low:high, :], w[:, cols])


def join_body(a, b, out):
    out[...] = (a[...] + b[...]).astype(BF16)


def final_body(fits, mine, other, across, s_mine, s_other, s_across, slow, s_slow, out, s_out):
    @pl.when(fits[0] == 1)
    def _():
        out[...] = (mine[...] + other[...] + across[...].astype(F32)).astype(BF16)
        s_out[...] = (s_mine[...] + s_other[...] + s_across[...].astype(F32)).astype(BF16)

    @pl.when(fits[0] != 1)
    def _():
        pltpu.sync_copy(slow, out)
        pltpu.sync_copy(s_slow, s_out)


def balanced(fits, queries, keys, values, out_weight, band_mask, positions, starts):
    rows, width = queries.shape
    seq_count = lax.axis_size("seq")
    head_count = lax.axis_size("head")
    rank = lax.axis_index("seq")
    place = lax.axis_index("head")
    blocks = rows // BLOCK
    total = positions.shape[0]
    home_rows = total // seq_count
    factor = (1.0 / math.sqrt(HEAD_DIM)) * math.log2(math.e)
    shape = jax.ShapeDtypeStruct

    def seq_pp(x, f):
        return lax.ppermute(x, "seq", [(i, f(i) % seq_count) for i in range(seq_count)])

    def head_pp(x, f):
        return lax.ppermute(x, "head", [(i, f(i) % head_count) for i in range(head_count)])

    edge = shape((BLOCK, 2 * width), BF16)

    pick = shape((SLOTS, 3 * width), BF16)
    keep, away = kernel_call(
        pick_body,
        [pick, pick],
        [rank[None].astype(jnp.int32), positions[None, :], queries, keys, values],
        [pltpu.VMEM((384, 8), F32)],
        smem=(0,),
    )
    first_kv, last_kv = kernel_call(edge_body, [edge, edge], [keys, values, keep], hbm=(2,))
    near = seq_pp(keep, lambda i: i ^ 1)

    line_count = head_count // 4
    side = jnp.stack([place % 2, place // 2 % 2]).astype(jnp.int32)
    cut = kernel_call(
        cut_body, shape((line_count, width, 4 * width), BF16), [out_weight, first_kv], hbm=(1,)
    )
    beside = seq_pp(away, lambda i: i ^ 2)
    beside, cut = lax.optimization_barrier((beside, cut))
    pair = keep + near + beside + seq_pp(away, lambda i: i ^ 3)
    weights = lax.all_to_all(
        cut,
        "head",
        0,
        0,
        axis_index_groups=[[4 * x + k for x in range(line_count)] for k in range(4)],
        tiled=True,
    )

    up = lambda x: seq_pp(x, lambda i: i + 2)
    down = lambda x: seq_pp(x, lambda i: i - 2)
    a1, b1 = up(pair), down(pair)
    a1, b1, fits = lax.optimization_barrier((a1, b1, fits))
    a2, b2 = up(a1), down(b1)
    a2, b2, first_kv, last_kv = lax.optimization_barrier((a2, b2, first_kv, last_kv))
    before = seq_pp(last_kv, lambda i: i + 1)
    after = seq_pp(first_kv, lambda i: i - 1)
    a3, b3 = up(a2), down(b2)
    half = SLOTS // 2
    a4, b4 = up(a3[:half]), down(b3[half:])
    a4, b4, weights = lax.optimization_barrier((a4, b4, weights))
    pieces = [pair, a1, b1, a2, b2, a3, b3, a4, b4]
    line = (rank // 2 + jnp.array([0, -1, 1, -2, 2, -3, 3, -4, -4], jnp.int32)) % (seq_count // 2)
    extra = jnp.array([0] * 8 + [half], jnp.int32)
    places = jnp.take(starts // 16 * 16, line // 2) + SLOTS * (line % 2) + extra

    offsets = jnp.arange(3, dtype=jnp.int32) - 1
    my_block = rank * blocks + jnp.arange(blocks, dtype=jnp.int32)
    neighbour = my_block[:, None] + offsets[None, :]
    live = (band_mask == 1) & (neighbour >= 0) & (neighbour < seq_count * blocks)
    relative = (positions // BLOCK)[None, :] - my_block[:, None]
    hits = (relative[:, None, :] == offsets[None, :, None]) & live[:, :, None]
    bias = jnp.where(jnp.any(hits, axis=1), jnp.float32(NEG), jnp.float32(0.0))[:, None, :]
    acc, stat, summary_queries = kernel_call(
        functools.partial(gather_body, factor, len(pieces)),
        [
            shape((rows, width), F32),
            shape((rows, HEAD_DIM), F32),
            shape((total, width), BF16),
        ],
        [places, queries, bias] + pieces,
        [
            pltpu.VMEM((total + 2 * SLOTS, width), BF16),
            pltpu.VMEM((total + 2 * SLOTS, width), BF16),
            pltpu.VMEM((total + 2 * SLOTS, width), BF16),
            pltpu.VMEM((total, 2 * width), BF16),
        ],
        smem=(0,),
    )
    attended = kernel_call(
        functools.partial(band_body, factor),
        shape((rows, width), BF16),
        [live.astype(jnp.int32), queries, keys, values, before, after, acc, stat],
        [pltpu.VMEM((rows + 2 * BLOCK, width), BF16), pltpu.VMEM((rows + 2 * BLOCK, 2 * width), BF16)],
        smem=(0,),
    )

    xu = lambda x: head_pp(x, lambda i: i + 4)
    xd = lambda x: head_pp(x, lambda i: i - 4)
    mid = rows // 2
    u1, d1 = xu(attended), xd(attended)

    partial = kernel_call(
        functools.partial(summary_body, factor),
        shape((total, width + CODE), BF16),
        [summary_queries, keys, values],
        [pltpu.VMEM((rows, 2 * width), BF16)],
    )
    sent = lax.all_to_all(
        partial.reshape(seq_count, home_rows, width + CODE), "seq", 0, 0, tiled=True
    )
    u2, d2 = xu(u1[:mid]), xd(d1[mid:])
    order = ((place // 4 - jnp.arange(line_count)) % line_count).astype(jnp.int32)

    def project(layout, flips, parts, count):
        full = shape((count, width), F32)
        return kernel_call(
            functools.partial(project_body, layout, flips),
            [full] * (2 * len(flips)),
            [side, order, *parts, weights],
            [
                pltpu.VMEM((count, line_count * width), BF16),
                pltpu.VMEM((line_count * width, 4 * width), BF16),
                pltpu.SemaphoreType.DMA((line_count,)),
            ],
            smem=(0, 1),
            hbm=(2 + len(layout),),
        )

    layout = [(0, 0), (0, 1), (0, 3), (0, 2), (mid, 2)]
    parts = [attended, u1, d1, u2, d2]
    mine, other = project(layout, (1,), parts, rows)
    other = head_pp(other, lambda i: i ^ 1)
    across = kernel_call(join_body, shape((rows, width), BF16), [mine, other])
    across, sent = lax.optimization_barrier((across, sent))
    across = head_pp(across, lambda i: i ^ 2)
    mine, other = project(layout, (0,), parts, rows)
    other = head_pp(other, lambda i: i ^ 1)

    own = kernel_call(merge_body, shape((home_rows, width), BF16), [sent])
    far = [head_pp(own, lambda i: i + 4 * d) for d in range(1, line_count)]
    s_layout = [(0, d) for d in range(line_count)]
    s_sums = project(s_layout, (1, 0), [own, *far], home_rows)
    s_other = head_pp(jnp.concatenate([s_sums[1], s_sums[3]], axis=0), lambda i: i ^ 1)
    s_other, across = lax.optimization_barrier((s_other, across))
    s_across = kernel_call(
        join_body, shape((home_rows, width), BF16), [s_sums[0], s_other[:home_rows]]
    )
    s_across = head_pp(s_across, lambda i: i ^ 2)
    return fits, mine, other, across, s_sums[2], s_other[home_rows:], s_across


def per_device(queries, keys, values, out_weight, band_mask, positions):
    rows, width = queries.shape
    seq_count = lax.axis_size("seq")
    edges = jnp.arange(seq_count // GROUP + 1, dtype=jnp.int32) * (GROUP * rows)
    starts = jnp.sum((positions[None, :] < edges[:, None]).astype(jnp.int32), axis=1, dtype=jnp.int32)
    fits = jnp.max(starts[1:] - starts[:-1] // 16 * 16) <= 2 * SLOTS
    args = (queries, keys, values, out_weight, band_mask, positions, starts)
    home_rows = positions.shape[0] // seq_count
    fits, *parts = balanced(fits.astype(jnp.int32), *args)
    slow = lax.cond(
        fits == 1,
        lambda *_: (jnp.zeros((rows, width), BF16), jnp.zeros((home_rows, width), BF16)),
        general,
        *args,
    )
    shape = jax.ShapeDtypeStruct
    return tuple(
        kernel_call(
            final_body,
            [shape((rows, width), BF16), shape((home_rows, width), BF16)],
            [fits[None], *parts, *slow],
            smem=(0,),
            hbm=(7, 8),
        )
    )


def solution(mesh):
    in_specs = (
        P("seq", "head"),
        P("seq", "head"),
        P("seq", "head"),
        P("head", None),
        P("seq", None),
        P(),
    )
    out_specs = (P("seq", "head"), P("seq", "head"))
    return jax.shard_map(
        per_device, mesh=mesh, in_specs=in_specs, out_specs=out_specs, check_vma=False
    )
```
